512 devices in a mesh: depth: 4 (over z_lo), row: 8 (over x, core), col: 16 (over z_hi, y).
Axes of the slice: x: 4, y: 4, z: 16 (z_hi: 4, z_lo: 4; z = z_hi * 4 + z_lo), core: 2. Of those that a mesh axis runs over, the one named last changes fastest.
Arguments:
- tokens: bfloat16 [512, 12288], P(('depth', 'col'), 'row'), may hold values from -6 to 6
- first_weight: bfloat16 [12288, 24576], P('row', ('depth', 'col')), may hold values from -0.0546875 to 0.0546875
- second_weight: bfloat16 [24576, 12288], P(('depth', 'col'), 'row'), may hold values from -0.0390625 to 0.0390625
- grad_out: bfloat16 [512, 12288], P(('depth', 'col'), 'row'), may hold values from -3 to 3
Outputs:
- block_out: bfloat16 [512, 12288], P(('depth', 'col'), 'row')
- input_grad: bfloat16 [512, 12288], P(('depth', 'col'), 'row')
- first_grad: bfloat16 [12288, 24576], P('row', ('depth', 'col'))
- second_grad: bfloat16 [24576, 12288], P(('depth', 'col'), 'row')
The draws below stay inside these ranges and needn't reach their ends.
All inputs are finite; a program needn't handle non-finite values.
Results may differ from the reference program's by a relative error of at most 0.0049.
Values may be sent and summed in bfloat16 or wider, within the bound.
No kernel may reach another device: no remote copies, remote signals or barrier semaphores. Data moves between devices by JAX's collectives and lax.ppermute only.
A program may use at most 64 MiB of HBM per device.

```python
import math
import jax
import jax.numpy as jnp

D = 12288
FF = 24576
TOKENS = 512


def level_of(stream_key, extent, split, least, largest):
    factor_of = 1.0
    for axis_at, shards_of in split:
        heights = jax.random.uniform(jax.random.fold_in(jax.random.fold_in(stream_key, 6), axis_at), (shards_of,), jnp.float32, least / len(split), largest / len(split))
        factor_of = factor_of * jnp.repeat(jnp.exp(heights), extent[axis_at] // shards_of).reshape((-1,) + (1,) * (len(extent) - 1 - axis_at))
    return factor_of


def gaussian(rng, dims, width, reach, pieces=(), dtype=jnp.bfloat16):
    level = level_of(rng, dims, pieces, -0.22, 0.18) if pieces else 1.0
    entries = jax.random.normal(rng, dims, jnp.float32) * width * level
    return jnp.minimum(jnp.maximum(entries, -reach), reach).astype(dtype)


def setup_inputs(seed: int = 0) -> dict:
    key_of = jax.random.split(jax.random.key(seed), 5)
    return {
        "tokens": gaussian(key_of[0], (TOKENS, D), 1.0, 6.0, ((0, 64), (1, 8))),
        "first_weight": gaussian(key_of[1], (D, FF), D ** -0.5, 0.0546875, ((0, 8), (1, 64))),
        "second_weight": gaussian(key_of[2], (FF, D), FF ** -0.5, 0.0390625, ((0, 64), (1, 8))),
        "grad_out": gaussian(key_of[3], (TOKENS, D), 0.5, 3.0, ((0, 64), (1, 8))),
    }


root_scale = math.sqrt(2.0 / math.pi)
cubic_coef = 0.044715

def gelu_value(values):
    tangent = jnp.tanh(root_scale * (values + cubic_coef * values * values * values))
    return 0.5 * values * (1.0 + tangent)

def gelu_slope(values):
    tangent = jnp.tanh(root_scale * (values + cubic_coef * values * values * values))
    return 0.5 * (1.0 + tangent) + 0.5 * values * (1.0 - tangent * tangent) * root_scale * (1.0 + 3.0 * cubic_coef * values * values)

def reference(tokens, first_weight, second_weight, grad_out):
    hidden_input = jnp.dot(tokens, first_weight, preferred_element_type=jnp.float32)
    hidden = gelu_value(hidden_input).astype(jnp.bfloat16)
    block_out = jnp.dot(hidden, second_weight, preferred_element_type=jnp.float32).astype(jnp.bfloat16)
    grad_hidden = jnp.dot(grad_out, second_weight.T, preferred_element_type=jnp.float32)
    grad_pre = (grad_hidden * gelu_slope(hidden_input)).astype(jnp.bfloat16)
    input_grad = jnp.dot(grad_pre, first_weight.T, preferred_element_type=jnp.float32).astype(jnp.bfloat16)
    first_grad = jnp.dot(tokens.T, grad_pre, preferred_element_type=jnp.float32).astype(jnp.bfloat16)
    second_grad = jnp.dot(hidden.T, grad_out, preferred_element_type=jnp.float32).astype(jnp.bfloat16)
    return (block_out, input_grad, first_grad, second_grad)
```

```python
import math

import jax
import jax.numpy as jnp
from jax import lax
from jax.sharding import Mesh, PartitionSpec as P

root_scale = math.sqrt(2.0 / math.pi)
cubic_coef = 0.044715

ROW = ("x", "core")


def gelu_pair(values):
    square = values * values
    tangent = jnp.tanh(root_scale * (values + cubic_coef * values * square))
    value = 0.5 * values * (1.0 + tangent)
    slope = 0.5 * (1.0 + tangent) + 0.5 * values * (1.0 - tangent * tangent) * root_scale * (
        1.0 + 3.0 * cubic_coef * square
    )
    return value, slope


def dot_over(left_side, right_side, left_dim, right_dim):
    return lax.dot_general(
        left_side,
        right_side,
        (((left_dim,), (right_dim,)), ((), ())),
        preferred_element_type=jnp.float32,
    )


def gather_rows(block, axis):
    size = lax.axis_size(axis)
    copies = jnp.broadcast_to(block[None], (size,) + block.shape)
    parts = lax.all_to_all(copies, axis, 0, 0)
    return parts.reshape(size * block.shape[0], block.shape[1])


def sum_rows(partial, axis):
    size = lax.axis_size(axis)
    rows, width = partial.shape
    parts = partial.astype(jnp.bfloat16).reshape(size, rows // size, width)
    parts = lax.all_to_all(parts, axis, 0, 0)
    return jnp.sum(parts.astype(jnp.float32), axis=0)


def on_device(tokens, first_weight, second_weight, grad_out):
    width = tokens.shape[1]
    units = first_weight.shape[1]
    both = jnp.concatenate([tokens, grad_out], axis=1)
    for axis in ("z_hi", "z_lo", "y"):
        both = gather_rows(both, axis)
    every_tokens, every_grads = both[:, :width], both[:, width:]
    partial = jnp.concatenate(
        [
            dot_over(every_tokens, first_weight, 1, 0).astype(jnp.bfloat16),
            dot_over(every_grads, second_weight, 1, 1).astype(jnp.bfloat16),
        ],
        axis=1,
    )
    summed = sum_rows(partial, ROW)
    hidden_share, slope = gelu_pair(summed[:, :units])
    pre_share = summed[:, units:] * slope
    shares = jnp.concatenate([hidden_share, pre_share], axis=1).astype(jnp.bfloat16)
    shares = gather_rows(shares, ROW)
    hidden, grad_pre = shares[:, :units], shares[:, units:]
    outs = jnp.concatenate(
        [
            dot_over(hidden, second_weight, 1, 0).astype(jnp.bfloat16),
            dot_over(grad_pre, first_weight, 1, 1).astype(jnp.bfloat16),
        ],
        axis=1,
    )
    first_grad = dot_over(every_tokens, grad_pre, 0, 0).astype(jnp.bfloat16)
    second_grad = dot_over(hidden, every_grads, 0, 0).astype(jnp.bfloat16)
    for axis in ("y", "z_lo", "z_hi"):
        outs = sum_rows(outs, axis)
    outs = outs.astype(jnp.bfloat16)
    return (outs[:, :width], outs[:, width:], first_grad, second_grad)


def solution(mesh):
    grid = Mesh(mesh.devices.reshape(4, 4, 2, 4, 4), ("z_lo", "x", "core", "z_hi", "y"))
    rows = P(("z_lo", "z_hi", "y"), ROW)
    columns = P(ROW, ("z_lo", "z_hi", "y"))
    return jax.shard_map(
        on_device,
        mesh=grid,
        in_specs=(rows, columns, rows, rows),
        out_specs=(rows, rows, columns, rows),
        check_vma=False,
    )
```

```python
import math

import jax
import jax.numpy as jnp
from jax import lax
from jax.experimental import pallas as pl
from jax.experimental.pallas import tpu as pltpu
from jax.sharding import Mesh, PartitionSpec as P

root_scale = math.sqrt(2.0 / math.pi)
cubic_coef = 0.044715

GRID = ("z_lo", "x", "core", "z_hi", "y")
SIZES = (4, 4, 2, 4, 4)
ROW = ("x", "core")
BLOCK = 32
PIECE = 128
HALF = 64
SWAP = ((0, 1), (1, 0))
params = pltpu.CompilerParams(vmem_limit_bytes=32 << 20)


def place_of(z_lo, x, core, z_hi, y):
    return (((z_lo * 4 + x) * 2 + core) * 4 + z_hi) * 4 + y


def every_place():
    for z_lo in range(4):
        for x in range(4):
            for core in range(2):
                for z_hi in range(4):
                    for y in range(4):
                        yield z_lo, x, core, z_hi, y


def near_groups():
    groups = []
    for x in range(4):
        for z_hi in range(4):
            for other in range(4):
                groups.append([place_of(i, x, 0, z_hi, other) for i in range(4)])
                groups.append([place_of(other, x, 1, z_hi, i) for i in range(4)])
    return groups


def far_shift(step):
    pairs = []
    for z_lo, x, core, z_hi, y in every_place():
        if core == 0:
            target = place_of(z_lo, x, core, z_hi, (y + step) % 4)
        else:
            z = (z_hi * 4 + z_lo + step) % 16
            target = place_of(z % 4, x, core, z // 4, y)
        pairs.append((place_of(z_lo, x, core, z_hi, y), target))
    return pairs


def moved(value, step):
    return lax.ppermute(value, GRID, far_shift(step))


def dot_over(left_side, right_side, left_dim, right_dim):
    return lax.dot_general(
        left_side,
        right_side,
        (((left_dim,), (right_dim,)), ((), ())),
        preferred_element_type=jnp.float32,
    )


def copies_of(block, count):
    return jnp.broadcast_to(block[None], (count,) + block.shape)


def common_block(core, own, piece, part):
    index = lax.rem(own + piece, 4)
    return jnp.where(core == 0, index * 4 + part, part * 4 + index)


def first_kernel(place, p0, p1, p2a, p2b, p3, first, second, both, kept, given, sums):
    core, own = place[0], place[1]
    width = first.shape[0]
    units = first.shape[1]
    both[0:128, :] = p0[...]
    both[128:256, :] = p1[...]
    both[256:320, :] = p2a[...]
    both[320:384, :] = p2b[...]
    both[384:512, :] = p3[...]
    sums[:, :units] = dot_over(both[:, :width], first[...], 1, 0)
    sums[:, units:] = dot_over(both[:, width:], second[...], 1, 1)
    for piece in range(4):
        for part in range(4):
            block = common_block(core, own, piece, part)
            start = pl.multiple_of(lax.rem(block, 8) * BLOCK, BLOCK)
            at = (piece * 4 + part) * BLOCK
            mine = block // 8 == core

            @pl.when(mine)
            def _():
                kept[pl.ds(start, BLOCK), :] = sums[at : at + BLOCK, :]

            @pl.when(jnp.logical_not(mine))
            def _():
                given[pl.ds(start, BLOCK), :] = sums[at : at + BLOCK, :]


def gelu_kernel(parts, shares):
    units = shares.shape[2] // 2
    total = parts[0] + parts[1] + parts[2] + parts[3]
    values, slopes = total[:, :units], total[:, units:]
    square = values * values
    tangent = jnp.tanh(root_scale * (values + cubic_coef * values * square))
    hidden = 0.5 * values * (1.0 + tangent)
    slope = 0.5 * (1.0 + tangent) + 0.5 * values * (1.0 - tangent * tangent) * root_scale * (
        1.0 + 3.0 * cubic_coef * square
    )
    pre = slopes * slope
    for copy in range(4):
        shares[copy, :, :units] = hidden.astype(jnp.bfloat16)
        shares[copy, :, units:] = pre.astype(jnp.bfloat16)


def second_kernel(place, shares, first, second, o0, o1, o2a, o2b, o3, local):
    core, own = place[0], place[1]
    width = first.shape[0]
    units = first.shape[1]
    for piece in range(4):
        for part in range(4):
            block = common_block(core, own, piece, part)
            start = pl.multiple_of(block * BLOCK, BLOCK)
            at = (piece * 4 + part) * BLOCK
            local[at : at + BLOCK, :] = shares[pl.ds(start, BLOCK), :]
    for side in range(2):
        rows = local[:, side * units : (side + 1) * units]
        if side == 0:
            outs = dot_over(rows, second[...], 1, 0)
        else:
            outs = dot_over(rows, first[...], 1, 1)
        columns = slice(side * width, (side + 1) * width)
        o0[:, columns] = outs[0:128]
        o1[:, columns] = outs[128:256].astype(jnp.bfloat16)
        o2a[:, columns] = outs[256:320].astype(jnp.bfloat16)
        o2b[:, columns] = outs[320:384].astype(jnp.bfloat16)
        o3[:, columns] = outs[384:512].astype(jnp.bfloat16)


def summed(parts):
    return jnp.sum(parts.astype(jnp.float32), axis=0).astype(jnp.bfloat16)


def shape_of(rows, columns, dtype):
    return jax.ShapeDtypeStruct((rows, columns), dtype)


def on_device(tokens, first_weight, second_weight, grad_out):
    width = tokens.shape[1]
    units = first_weight.shape[1]
    core = lax.axis_index("core")
    own = jnp.where(core == 0, lax.axis_index("y"), lax.axis_index("z_lo"))
    place = jnp.stack([core, own]).astype(jnp.int32)
    scalars = pl.BlockSpec(memory_space=pltpu.SMEM)
    whole = pl.BlockSpec(memory_space=pltpu.VMEM)
    near = near_groups()

    both = jnp.concatenate([tokens, grad_out], axis=1)
    both = lax.all_to_all(copies_of(both, 4), "z_hi", 0, 0).reshape(BLOCK, 2 * width)
    both = lax.all_to_all(copies_of(both, 4), GRID, 0, 0, axis_index_groups=near)
    both = both.reshape(PIECE, 2 * width)
    p1 = moved(both, -1)
    p3 = moved(both, 1)
    p2a = moved(both[:HALF], -2)
    p2b = moved(both[HALF:], 2)

    every, kept, given = pl.pallas_call(
        first_kernel,
        out_shape=(
            shape_of(512, 2 * width, jnp.bfloat16),
            shape_of(256, 2 * units, jnp.float32),
            shape_of(256, 2 * units, jnp.float32),
        ),
        in_specs=[scalars] + [whole] * 7,
        out_specs=(whole, whole, whole),
        scratch_shapes=[pltpu.VMEM((512, 2 * units), jnp.float32)],
        compiler_params=params,
    )(place, both, p1, p2a, p2b, p3, first_weight, second_weight)
    kept = kept + lax.ppermute(given, "core", SWAP)
    parts = lax.all_to_all(kept.reshape(4, HALF, 2 * units), "x", 0, 0)
    shares = pl.pallas_call(
        gelu_kernel,
        out_shape=jax.ShapeDtypeStruct((4, HALF, 2 * units), jnp.bfloat16),
        in_specs=[whole],
        out_specs=whole,
        compiler_params=params,
    )(parts)
    shares = lax.all_to_all(shares, "x", 0, 0).reshape(256, 2 * units)
    shares = lax.all_gather(shares, "core", axis=0, tiled=True)
    o0, o1, o2a, o2b, o3, local = pl.pallas_call(
        second_kernel,
        out_shape=(
            shape_of(PIECE, 2 * width, jnp.float32),
            shape_of(PIECE, 2 * width, jnp.bfloat16),
            shape_of(HALF, 2 * width, jnp.bfloat16),
            shape_of(HALF, 2 * width, jnp.bfloat16),
            shape_of(PIECE, 2 * width, jnp.bfloat16),
            shape_of(512, 2 * units, jnp.bfloat16),
        ),
        in_specs=[scalars] + [whole] * 3,
        out_specs=(whole,) * 6,
        compiler_params=params,
    )(place, shares, first_weight, second_weight)
    r1 = moved(o1, 1)
    r3 = moved(o3, -1)
    r2a = moved(o2a, 2)
    r2b = moved(o2b, -2)
    hidden, grad_pre = local[:, :units], local[:, units:]
    first_grad = dot_over(every[:, :width], grad_pre, 0, 0).astype(jnp.bfloat16)
    second_grad = dot_over(hidden, every[:, width:], 0, 0).astype(jnp.bfloat16)
    r2 = jnp.concatenate([r2a, r2b], axis=0)
    outs = o0 + r1.astype(jnp.float32) + r3.astype(jnp.float32) + r2.astype(jnp.float32)
    outs = outs.astype(jnp.bfloat16).reshape(4, BLOCK, 2 * width)
    outs = summed(lax.all_to_all(outs, GRID, 0, 0, axis_index_groups=near))
    outs = summed(lax.all_to_all(outs.reshape(4, 8, 2 * width), "z_hi", 0, 0))
    return (outs[:, :width], outs[:, width:], first_grad, second_grad)


def solution(mesh):
    grid = Mesh(mesh.devices.reshape(SIZES), GRID)
    rows = P(("z_lo", "z_hi", "y"), ROW)
    columns = P(ROW, ("z_lo", "z_hi", "y"))
    return jax.shard_map(
        on_device,
        mesh=grid,
        in_specs=(rows, columns, rows, rows),
        out_specs=(rows, rows, columns, rows),
        check_vma=False,
    )
```

```python
import math

import jax
import jax.numpy as jnp
from jax import lax
from jax.experimental import pallas as pl
from jax.experimental.pallas import tpu as pltpu
from jax.sharding import Mesh, PartitionSpec as P

root_scale = math.sqrt(2.0 / math.pi)
cubic_coef = 0.044715

GRID = ("z_lo", "x", "core", "z_hi", "y")
SIZES = (4, 4, 2, 4, 4)
ROW = ("x", "core")
SWAP = ((0, 1), (1, 0))
BLOCK = 32
PIECE = 128
SHARE = 64
LONG = 64
SHORT = PIECE - LONG
ORDER = (0, 1, 3, 2)
params = pltpu.CompilerParams(vmem_limit_bytes=20 << 20)


def place_of(z_lo, x, core, z_hi, y):
    return (((z_lo * 4 + x) * 2 + core) * 4 + z_hi) * 4 + y


def every_place():
    for z_lo in range(4):
        for x in range(4):
            for core in range(2):
                for z_hi in range(4):
                    for y in range(4):
                        yield z_lo, x, core, z_hi, y


def near_groups():
    groups = []
    for x in range(4):
        for z_hi in range(4):
            for other in range(4):
                groups.append([place_of(i, x, 0, z_hi, other) for i in range(4)])
                groups.append([place_of(other, x, 1, z_hi, i) for i in range(4)])
    return groups


def far_shift(step):
    pairs = []
    for z_lo, x, core, z_hi, y in every_place():
        if core == 0:
            target = place_of(z_lo, x, core, z_hi, (y + step) % 4)
        else:
            z = (z_hi * 4 + z_lo + step) % 16
            target = place_of(z % 4, x, core, z // 4, y)
        pairs.append((place_of(z_lo, x, core, z_hi, y), target))
    return pairs


def moved(value, step):
    return lax.ppermute(value, GRID, far_shift(step))


def dot_over(left_side, right_side, left_dim, right_dim):
    return lax.dot_general(
        left_side,
        right_side,
        (((left_dim,), (right_dim,)), ((), ())),
        preferred_element_type=jnp.float32,
    )


def copies_of(block, count):
    return jnp.broadcast_to(block[None], (count,) + block.shape)


def common_block(core, own, piece, part):
    index = lax.rem(own + piece, 4)
    return jnp.where(core == 0, index * 4 + part, part * 4 + index)


def first_kernel(p0, first, second, sums):
    width = first.shape[0]
    units = first.shape[1]
    sums[:, :units] = dot_over(p0[:, :width], first[...], 1, 0)
    sums[:, units:] = dot_over(p0[:, width:], second[...], 1, 1)


def last_kernel(place, sums, p1, p3, p2a, p2b, first, second, both, kept, given, rest):
    core, own = place[0], place[1]
    width = first.shape[0]
    units = first.shape[1]
    both[0:128, :] = p1[...]
    both[128:256, :] = p3[...]
    both[256 : 256 + SHORT, :] = p2a[...]
    both[256 + SHORT : 384, :] = p2b[...]
    rest[:, :units] = dot_over(both[:, :width], first[...], 1, 0)
    rest[:, units:] = dot_over(both[:, width:], second[...], 1, 1)
    for slot in range(4):
        source, base = (sums, 0) if slot == 0 else (rest, PIECE)
        for part in range(4):
            block = common_block(core, own, ORDER[slot], part)
            start = pl.multiple_of(lax.rem(block, 8) * BLOCK, BLOCK)
            at = (slot * 4 + part) * BLOCK - base
            mine = block // 8 == core

            @pl.when(mine)
            def _():
                kept[pl.ds(start, BLOCK), :] = source[at : at + BLOCK, :]

            @pl.when(jnp.logical_not(mine))
            def _():
                given[pl.ds(start, BLOCK), :] = source[at : at + BLOCK, :]


def add_kernel(kept, more, total, sent):
    values = kept[...] + more[...]
    total[...] = values
    sent[...] = values.astype(jnp.bfloat16)


def lost(values):
    return values - values.astype(jnp.bfloat16).astype(jnp.float32)


def total_of(parts, own_lost):
    wide = [parts[i].astype(jnp.float32) for i in range(4)]
    return ((wide[0] + wide[1]) + (wide[2] + wide[3])) + own_lost


def gelu_kernel(place, parts, kept, shares):
    units = shares.shape[2] // 2
    total = total_of(parts, lost(kept[place[2]]))
    values, slopes = total[:, :units], total[:, units:]
    square = values * values
    tangent = jnp.tanh(root_scale * (values + cubic_coef * values * square))
    hidden = 0.5 * values * (1.0 + tangent)
    slope = 0.5 * (1.0 + tangent) + 0.5 * values * (1.0 - tangent * tangent) * root_scale * (
        1.0 + 3.0 * cubic_coef * square
    )
    pre = slopes * slope
    for copy in range(4):
        shares[copy, :, :units] = hidden.astype(jnp.bfloat16)
        shares[copy, :, units:] = pre.astype(jnp.bfloat16)


def out_rows(rows, first, second):
    units = first.shape[1]
    return (
        dot_over(rows[:, :units], second[...], 1, 0),
        dot_over(rows[:, units:], first[...], 1, 1),
    )


def second_kernel(place, shares, first, second, o1, o2a, o2b, o3, local):
    core, own = place[0], place[1]
    width = first.shape[0]
    for slot in range(4):
        for part in range(4):
            block = common_block(core, own, ORDER[slot], part)
            start = pl.multiple_of(block * BLOCK, BLOCK)
            at = (slot * 4 + part) * BLOCK
            local[at : at + BLOCK, :] = shares[pl.ds(start, BLOCK), :]
    sides = out_rows(local[128:512, :], first, second)
    for side in range(2):
        outs = sides[side].astype(jnp.bfloat16)
        columns = slice(side * width, (side + 1) * width)
        o1[:, columns] = outs[0:128]
        o3[:, columns] = outs[128:256]
        o2a[:, columns] = outs[256 : 256 + LONG]
        o2b[:, columns] = outs[256 + LONG : 384]


def own_kernel(local, first, second, o0):
    width = first.shape[0]
    sides = out_rows(local[0:128, :], first, second)
    o0[:, :width] = sides[0]
    o0[:, width:] = sides[1]


def far_kernel(place, o0, r1, r2a, r2b, r3, outs, own_lost):
    for part in range(4):
        rows = slice(part * BLOCK, (part + 1) * BLOCK)
        if part < 2:
            r2 = r2a[rows, :]
        else:
            r2 = r2b[part * BLOCK - LONG : part * BLOCK - LONG + BLOCK, :]
        total = o0[rows, :] + r1[rows, :].astype(jnp.float32)
        total = total + r3[rows, :].astype(jnp.float32) + r2.astype(jnp.float32)
        outs[part] = total.astype(jnp.bfloat16)

        @pl.when(place[3] == part)
        def _():
            own_lost[...] = lost(total)


def near_kernel(place, parts, own_lost, outs, next_lost):
    total = total_of(parts, own_lost[...])
    outs[...] = total.astype(jnp.bfloat16)
    for part in range(4):

        @pl.when(place[4] == part)
        def _():
            next_lost[...] = lost(total[part * 8 : part * 8 + 8, :])


def end_kernel(parts, own_lost, block_out, input_grad):
    width = block_out.shape[1]
    outs = total_of(parts, own_lost[...]).astype(jnp.bfloat16)
    block_out[...] = outs[:, :width]
    input_grad[...] = outs[:, width:]


def shape_of(rows, columns, dtype):
    return jax.ShapeDtypeStruct((rows, columns), dtype)


def cost_of(rows):
    return pl.CostEstimate(
        flops=4 * rows * 1536 * 384, bytes_accessed=rows * 12288 + 2400000, transcendentals=0
    )


def on_device(tokens, first_weight, second_weight, grad_out):
    width = tokens.shape[1]
    units = first_weight.shape[1]
    core = lax.axis_index("core")
    y, z_lo = lax.axis_index("y"), lax.axis_index("z_lo")
    own, other = jnp.where(core == 0, y, z_lo), jnp.where(core == 0, z_lo, y)
    x, z_hi = lax.axis_index("x"), lax.axis_index("z_hi")
    place = jnp.stack([core, own, x, other, z_hi]).astype(jnp.int32)
    scalars = pl.BlockSpec(memory_space=pltpu.SMEM)
    whole = pl.BlockSpec(memory_space=pltpu.VMEM)
    near = near_groups()

    both = jnp.concatenate([tokens, grad_out], axis=1)
    both = lax.all_to_all(copies_of(both, 4), "z_hi", 0, 0).reshape(BLOCK, 2 * width)
    both = lax.all_to_all(copies_of(both, 4), GRID, 0, 0, axis_index_groups=near)
    both = both.reshape(PIECE, 2 * width)
    p3 = moved(both, 1)
    p1 = moved(both, -1)
    p2b = moved(both[SHORT:], 2)
    p2a = moved(both[:SHORT], -2)

    sums = pl.pallas_call(
        first_kernel,
        out_shape=shape_of(PIECE, 2 * units, jnp.float32),
        in_specs=[whole] * 3,
        out_specs=whole,
        compiler_params=params,
        cost_estimate=cost_of(128),
    )(both, first_weight, second_weight)
    every, kept, given = pl.pallas_call(
        last_kernel,
        out_shape=(
            shape_of(384, 2 * width, jnp.bfloat16),
            shape_of(256, 2 * units, jnp.float32),
            shape_of(256, 2 * units, jnp.float32),
        ),
        in_specs=[scalars] + [whole] * 7,
        out_specs=(whole, whole, whole),
        scratch_shapes=[pltpu.VMEM((384, 2 * units), jnp.float32)],
        compiler_params=params,
        cost_estimate=cost_of(384),
    )(place, sums, p1, p3, p2a, p2b, first_weight, second_weight)
    kept, sent = pl.pallas_call(
        add_kernel,
        out_shape=(
            shape_of(256, 2 * units, jnp.float32),
            shape_of(256, 2 * units, jnp.bfloat16),
        ),
        in_specs=[whole] * 2,
        out_specs=(whole, whole),
        compiler_params=params,
    )(kept, lax.ppermute(given, "core", SWAP))
    parts = lax.all_to_all(sent.reshape(4, SHARE, 2 * units), "x", 0, 0)
    shares = pl.pallas_call(
        gelu_kernel,
        out_shape=jax.ShapeDtypeStruct((4, SHARE, 2 * units), jnp.bfloat16),
        in_specs=[scalars, whole, whole],
        out_specs=whole,
        compiler_params=params,
    )(place, parts, kept.reshape(4, SHARE, 2 * units))
    shares = lax.all_to_all(shares, "x", 0, 0).reshape(256, 2 * units)
    shares = lax.all_gather(shares, "core", axis=0, tiled=True)
    o1, o2a, o2b, o3, local = pl.pallas_call(
        second_kernel,
        out_shape=(
            shape_of(PIECE, 2 * width, jnp.bfloat16),
            shape_of(LONG, 2 * width, jnp.bfloat16),
            shape_of(SHORT, 2 * width, jnp.bfloat16),
            shape_of(PIECE, 2 * width, jnp.bfloat16),
            shape_of(512, 2 * units, jnp.bfloat16),
        ),
        in_specs=[scalars] + [whole] * 3,
        out_specs=(whole,) * 5,
        compiler_params=params,
        cost_estimate=cost_of(384),
    )(place, shares, first_weight, second_weight)
    r1 = moved(o1, 1)
    r3 = moved(o3, -1)
    r2a = moved(o2a, 2)
    r2b = moved(o2b, -2)
    o0 = pl.pallas_call(
        own_kernel,
        out_shape=shape_of(PIECE, 2 * width, jnp.float32),
        in_specs=[whole] * 3,
        out_specs=whole,
        compiler_params=params,
        cost_estimate=cost_of(128),
    )(local, first_weight, second_weight)
    hidden, grad_pre = local[:, :units], local[:, units:]
    first_grad = dot_over(every[:, :width], grad_pre[PIECE:], 0, 0)
    first_grad = first_grad + dot_over(both[:, :width], grad_pre[:PIECE], 0, 0)
    second_grad = dot_over(hidden[PIECE:], every[:, width:], 0, 0)
    second_grad = second_grad + dot_over(hidden[:PIECE], both[:, width:], 0, 0)
    first_grad = first_grad.astype(jnp.bfloat16)
    second_grad = second_grad.astype(jnp.bfloat16)
    o0, first_grad, second_grad = lax.optimization_barrier((o0, first_grad, second_grad))
    outs, own_lost = pl.pallas_call(
        far_kernel,
        out_shape=(
            jax.ShapeDtypeStruct((4, BLOCK, 2 * width), jnp.bfloat16),
            shape_of(BLOCK, 2 * width, jnp.float32),
        ),
        in_specs=[scalars] + [whole] * 5,
        out_specs=(whole, whole),
        compiler_params=params,
    )(place, o0, r1, r2a, r2b, r3)
    outs = lax.all_to_all(outs, GRID, 0, 0, axis_index_groups=near)
    outs, own_lost = pl.pallas_call(
        near_kernel,
        out_shape=(
            shape_of(BLOCK, 2 * width, jnp.bfloat16),
            shape_of(8, 2 * width, jnp.float32),
        ),
        in_specs=[scalars, whole, whole],
        out_specs=(whole, whole),
        compiler_params=params,
    )(place, outs, own_lost)
    outs = lax.all_to_all(outs.reshape(4, 8, 2 * width), "z_hi", 0, 0)
    block_out, input_grad = pl.pallas_call(
        end_kernel,
        out_shape=(shape_of(8, width, jnp.bfloat16), shape_of(8, width, jnp.bfloat16)),
        in_specs=[whole, whole],
        out_specs=(whole, whole),
        compiler_params=params,
    )(outs, own_lost)
    return (block_out, input_grad, first_grad, second_grad)


def solution(mesh):
    grid = Mesh(mesh.devices.reshape(SIZES), GRID)
    rows = P(("z_lo", "z_hi", "y"), ROW)
    columns = P(ROW, ("z_lo", "z_hi", "y"))
    return jax.shard_map(
        on_device,
        mesh=grid,
        in_specs=(rows, columns, rows, rows),
        out_specs=(rows, rows, columns, rows),
        check_vma=False,
    )
```

```python
import math

import jax
import jax.numpy as jnp
from jax import lax
from jax.experimental import pallas as pl
from jax.experimental.pallas import tpu as pltpu
from jax.sharding import Mesh, PartitionSpec as P

root_scale = math.sqrt(2.0 / math.pi)
cubic_coef = 0.044715

GRID = ("z_lo", "x", "core", "z_hi", "y")
SIZES = (4, 4, 2, 4, 4)
ROW = ("x", "core")
SWAP = ((0, 1), (1, 0))
BLOCK = 32
PIECE = 128
SHARE = 64
params = pltpu.CompilerParams(vmem_limit_bytes=20 << 20)


def place_of(z_lo, x, core, z_hi, y):
    return (((z_lo * 4 + x) * 2 + core) * 4 + z_hi) * 4 + y


def every_place():
    for z_lo in range(4):
        for x in range(4):
            for core in range(2):
                for z_hi in range(4):
                    for y in range(4):
                        yield z_lo, x, core, z_hi, y


def pair_groups():
    groups = []
    for x in range(4):
        for core in range(2):
            for z in range(0, 16, 2):
                for y in range(0, 4, 2):
                    group = []
                    for part in range(4):
                        real_z = (z + part // 2 + 1 - core) % 16
                        real_y = (y + part % 2 + 1 - core) % 4
                        group.append(place_of(real_z % 4, x, core, real_z // 4, real_y))
                    groups.append(group)
    return groups


def swapped(place, size):
    return (place + 1 if place % 2 else place - 1) % size


def moved(value, slot):
    pairs = []
    for z_lo, x, core, z_hi, y in every_place():
        shift = 1 - core
        z = (z_hi * 4 + z_lo - shift) % 16
        other_y, other_z = (y - shift) % 4, z
        if slot % 2:
            other_y = swapped(other_y, 4)
        if slot // 2:
            other_z = swapped(z, 16)
        other_y, other_z = (other_y + shift) % 4, (other_z + shift) % 16
        target = place_of(other_z % 4, x, core, other_z // 4, other_y)
        pairs.append((place_of(z_lo, x, core, z_hi, y), target))
    return lax.ppermute(value, GRID, pairs)


def dot_over(left_side, right_side, left_dim, right_dim):
    return lax.dot_general(
        left_side,
        right_side,
        (((left_dim,), (right_dim,)), ((), ())),
        preferred_element_type=jnp.float32,
    )


def copies_of(block, count):
    return jnp.broadcast_to(block[None], (count,) + block.shape)


def common_block(core, own, slot, part):
    pair = lax.bitwise_xor(own, jnp.int32(slot))
    shift = 1 - core
    y = lax.rem(lax.rem(pair, 2) * 2 + part % 2 + shift, 4)
    z = lax.rem(pair // 2 * 2 + part // 2 + shift, 4)
    return y * 4 + z


def first_kernel(p0, first, second, sums):
    width = first.shape[0]
    units = first.shape[1]
    sums[:, :units] = dot_over(p0[:, :width], first[...], 1, 0)
    sums[:, units:] = dot_over(p0[:, width:], second[...], 1, 1)


def last_kernel(place, p3, p1, p2, sums, first, second, both, kept, given, rest):
    core, own = place[0], place[1]
    width = first.shape[0]
    units = first.shape[1]
    both[0:128, :] = p1[...]
    both[128:256, :] = p2[...]
    both[256:384, :] = p3[...]
    rest[:, :units] = dot_over(both[:, :width], first[...], 1, 0)
    rest[:, units:] = dot_over(both[:, width:], second[...], 1, 1)
    for slot in range(4):
        source, base = (sums, 0) if slot == 0 else (rest, PIECE)
        for part in range(4):
            block = common_block(core, own, slot, part)
            start = pl.multiple_of(lax.rem(block, 8) * BLOCK, BLOCK)
            at = (slot * 4 + part) * BLOCK - base
            mine = block // 8 == core

            @pl.when(mine)
            def _():
                kept[pl.ds(start, BLOCK), :] = source[at : at + BLOCK, :]

            @pl.when(jnp.logical_not(mine))
            def _():
                given[pl.ds(start, BLOCK), :] = source[at : at + BLOCK, :]


def add_kernel(kept, more, total, sent):
    values = kept[...] + more[...]
    total[...] = values
    sent[...] = values.astype(jnp.bfloat16)


def lost(values):
    return values - values.astype(jnp.bfloat16).astype(jnp.float32)


def total_of(parts, own_lost):
    wide = [parts[i].astype(jnp.float32) for i in range(4)]
    return ((wide[0] + wide[1]) + (wide[2] + wide[3])) + own_lost


def gelu_kernel(place, parts, kept, shares):
    units = shares.shape[2] // 2
    total = total_of(parts, lost(kept[place[2]]))
    values, slopes = total[:, :units], total[:, units:]
    square = values * values
    tangent = jnp.tanh(root_scale * (values + cubic_coef * values * square))
    hidden = 0.5 * values * (1.0 + tangent)
    slope = 0.5 * (1.0 + tangent) + 0.5 * values * (1.0 - tangent * tangent) * root_scale * (
        1.0 + 3.0 * cubic_coef * square
    )
    pre = slopes * slope
    for copy in range(4):
        shares[copy, :, :units] = hidden.astype(jnp.bfloat16)
        shares[copy, :, units:] = pre.astype(jnp.bfloat16)


def out_rows(rows, first, second):
    units = first.shape[1]
    return (
        dot_over(rows[:, :units], second[...], 1, 0),
        dot_over(rows[:, units:], first[...], 1, 1),
    )


def second_kernel(place, shares, first, second, o1, o2, o3, local):
    core, own = place[0], place[1]
    width = first.shape[0]
    for slot in range(4):
        for part in range(4):
            block = common_block(core, own, slot, part)
            start = pl.multiple_of(block * BLOCK, BLOCK)
            at = (slot * 4 + part) * BLOCK
            local[at : at + BLOCK, :] = shares[pl.ds(start, BLOCK), :]
    sides = out_rows(local[128:512, :], first, second)
    for side in range(2):
        outs = sides[side].astype(jnp.bfloat16)
        columns = slice(side * width, (side + 1) * width)
        o1[:, columns] = outs[0:128]
        o2[:, columns] = outs[128:256]
        o3[:, columns] = outs[256:384]


def own_kernel(local, first, second, o0):
    width = first.shape[0]
    sides = out_rows(local[0:128, :], first, second)
    o0[:, :width] = sides[0]
    o0[:, width:] = sides[1]


def far_kernel(place, r3, r1, r2, o0, outs, own_lost):
    for part in range(4):
        rows = slice(part * BLOCK, (part + 1) * BLOCK)
        total = o0[rows, :] + r1[rows, :].astype(jnp.float32)
        total = total + r2[rows, :].astype(jnp.float32) + r3[rows, :].astype(jnp.float32)
        outs[part] = total.astype(jnp.bfloat16)

        @pl.when(place[3] == part)
        def _():
            own_lost[...] = lost(total)


def near_kernel(place, parts, own_lost, outs, next_lost):
    total = total_of(parts, own_lost[...])
    outs[...] = total.astype(jnp.bfloat16)
    for part in range(4):

        @pl.when(place[4] == part)
        def _():
            next_lost[...] = lost(total[part * 8 : part * 8 + 8, :])


def end_kernel(parts, own_lost, block_out, input_grad):
    width = block_out.shape[1]
    outs = total_of(parts, own_lost[...]).astype(jnp.bfloat16)
    block_out[...] = outs[:, :width]
    input_grad[...] = outs[:, width:]


def shape_of(rows, columns, dtype):
    return jax.ShapeDtypeStruct((rows, columns), dtype)


def cost_of(rows):
    return pl.CostEstimate(
        flops=4 * rows * 1536 * 384, bytes_accessed=rows * 12288 + 2400000, transcendentals=0
    )


def on_device(tokens, first_weight, second_weight, grad_out):
    width = tokens.shape[1]
    units = first_weight.shape[1]
    core, x = lax.axis_index("core"), lax.axis_index("x")
    y, z_lo, z_hi = lax.axis_index("y"), lax.axis_index("z_lo"), lax.axis_index("z_hi")
    y, z_lo = (y + 3 + core) % 4, (z_lo + 3 + core) % 4
    own, part = z_lo // 2 * 2 + y // 2, z_lo % 2 * 2 + y % 2
    place = jnp.stack([core, own, x, part, z_hi]).astype(jnp.int32)
    scalars = pl.BlockSpec(memory_space=pltpu.SMEM)
    whole = pl.BlockSpec(memory_space=pltpu.VMEM)
    near = pair_groups()

    both = jnp.concatenate([tokens, grad_out], axis=1)
    both = lax.all_to_all(copies_of(both, 4), "z_hi", 0, 0).reshape(BLOCK, 2 * width)
    both = lax.all_to_all(copies_of(both, 4), GRID, 0, 0, axis_index_groups=near)
    both = both.reshape(PIECE, 2 * width)
    p3, p1, p2 = moved(both, 3), moved(both, 1), moved(both, 2)

    sums = pl.pallas_call(
        first_kernel,
        out_shape=shape_of(PIECE, 2 * units, jnp.float32),
        in_specs=[whole] * 3,
        out_specs=whole,
        compiler_params=params,
        cost_estimate=cost_of(128),
    )(both, first_weight, second_weight)
    every, kept, given = pl.pallas_call(
        last_kernel,
        out_shape=(
            shape_of(384, 2 * width, jnp.bfloat16),
            shape_of(256, 2 * units, jnp.float32),
            shape_of(256, 2 * units, jnp.float32),
        ),
        in_specs=[scalars] + [whole] * 6,
        out_specs=(whole, whole, whole),
        scratch_shapes=[pltpu.VMEM((384, 2 * units), jnp.float32)],
        compiler_params=params,
        cost_estimate=cost_of(384),
    )(place, p3, p1, p2, sums, first_weight, second_weight)
    kept, sent = pl.pallas_call(
        add_kernel,
        out_shape=(
            shape_of(256, 2 * units, jnp.float32),
            shape_of(256, 2 * units, jnp.bfloat16),
        ),
        in_specs=[whole] * 2,
        out_specs=(whole, whole),
        compiler_params=params,
    )(kept, lax.ppermute(given, "core", SWAP))
    parts = lax.all_to_all(sent.reshape(4, SHARE, 2 * units), "x", 0, 0)
    shares = pl.pallas_call(
        gelu_kernel,
        out_shape=jax.ShapeDtypeStruct((4, SHARE, 2 * units), jnp.bfloat16),
        in_specs=[scalars, whole, whole],
        out_specs=whole,
        compiler_params=params,
    )(place, parts, kept.reshape(4, SHARE, 2 * units))
    shares = lax.all_to_all(shares, "x", 0, 0).reshape(256, 2 * units)
    shares = lax.all_gather(shares, "core", axis=0, tiled=True)
    o1, o2, o3, local = pl.pallas_call(
        second_kernel,
        out_shape=(
            shape_of(PIECE, 2 * width, jnp.bfloat16),
            shape_of(PIECE, 2 * width, jnp.bfloat16),
            shape_of(PIECE, 2 * width, jnp.bfloat16),
            shape_of(512, 2 * units, jnp.bfloat16),
        ),
        in_specs=[scalars] + [whole] * 3,
        out_specs=(whole,) * 4,
        compiler_params=params,
        cost_estimate=cost_of(384),
    )(place, shares, first_weight, second_weight)
    r3, r1, r2 = moved(o3, 3), moved(o1, 1), moved(o2, 2)
    o0 = pl.pallas_call(
        own_kernel,
        out_shape=shape_of(PIECE, 2 * width, jnp.float32),
        in_specs=[whole] * 3,
        out_specs=whole,
        compiler_params=params,
        cost_estimate=cost_of(128),
    )(local, first_weight, second_weight)
    hidden, grad_pre = local[:, :units], local[:, units:]
    first_grad = dot_over(every[:, :width], grad_pre[PIECE:], 0, 0)
    first_grad = first_grad + dot_over(both[:, :width], grad_pre[:PIECE], 0, 0)
    second_grad = dot_over(hidden[PIECE:], every[:, width:], 0, 0)
    second_grad = second_grad + dot_over(hidden[:PIECE], both[:, width:], 0, 0)
    first_grad = first_grad.astype(jnp.bfloat16)
    second_grad = second_grad.astype(jnp.bfloat16)
    o0, first_grad, second_grad = lax.optimization_barrier((o0, first_grad, second_grad))
    outs, own_lost = pl.pallas_call(
        far_kernel,
        out_shape=(
            jax.ShapeDtypeStruct((4, BLOCK, 2 * width), jnp.bfloat16),
            shape_of(BLOCK, 2 * width, jnp.float32),
        ),
        in_specs=[scalars] + [whole] * 4,
        out_specs=(whole, whole),
        compiler_params=params,
    )(place, r3, r1, r2, o0)
    outs = lax.all_to_all(outs, GRID, 0, 0, axis_index_groups=near)
    outs, own_lost = pl.pallas_call(
        near_kernel,
        out_shape=(
            shape_of(BLOCK, 2 * width, jnp.bfloat16),
            shape_of(8, 2 * width, jnp.float32),
        ),
        in_specs=[scalars, whole, whole],
        out_specs=(whole, whole),
        compiler_params=params,
    )(place, outs, own_lost)
    outs = lax.all_to_all(outs.reshape(4, 8, 2 * width), "z_hi", 0, 0)
    block_out, input_grad = pl.pallas_call(
        end_kernel,
        out_shape=(shape_of(8, width, jnp.bfloat16), shape_of(8, width, jnp.bfloat16)),
        in_specs=[whole, whole],
        out_specs=(whole, whole),
        compiler_params=params,
    )(outs, own_lost)
    return (block_out, input_grad, first_grad, second_grad)


def solution(mesh):
    grid = Mesh(mesh.devices.reshape(SIZES), GRID)
    rows = P(("z_lo", "z_hi", "y"), ROW)
    columns = P(ROW, ("z_lo", "z_hi", "y"))
    return jax.shard_map(
        on_device,
        mesh=grid,
        in_specs=(rows, columns, rows, rows),
        out_specs=(rows, rows, columns, rows),
        check_vma=False,
    )
```

```python
import math

import jax
import jax.numpy as jnp
from jax import lax
from jax.experimental import pallas as pl
from jax.experimental.pallas import tpu as pltpu
from jax.sharding import Mesh, PartitionSpec as P

root_scale = math.sqrt(2.0 / math.pi)
cubic_coef = 0.044715

GRID = ("z_lo", "x", "core", "z_hi", "y")
SIZES = (4, 4, 2, 4, 4)
ROW = ("x", "core")
SWAP = ((0, 1), (1, 0))
BLOCK = 32
PIECE = 128
SHARE = 64
params = pltpu.CompilerParams(vmem_limit_bytes=20 << 20)


def place_of(z_lo, x, core, z_hi, y):
    return (((z_lo * 4 + x) * 2 + core) * 4 + z_hi) * 4 + y


def every_place():
    for z_lo in range(4):
        for x in range(4):
            for core in range(2):
                for z_hi in range(4):
                    for y in range(4):
                        yield z_lo, x, core, z_hi, y


def pair_groups():
    groups = []
    for x in range(4):
        for core in range(2):
            for z in range(0, 16, 2):
                for y in range(0, 4, 2):
                    group = []
                    for part in range(4):
                        real_z = (z + part // 2 + 1 - core) % 16
                        real_y = (y + part % 2 + 1 - core) % 4
                        group.append(place_of(real_z % 4, x, core, real_z // 4, real_y))
                    groups.append(group)
    return groups


def swapped(place, size):
    return (place + 1 if place % 2 else place - 1) % size


def moved(value, slot):
    pairs = []
    for z_lo, x, core, z_hi, y in every_place():
        shift = 1 - core
        z = (z_hi * 4 + z_lo - shift) % 16
        other_y, other_z = (y - shift) % 4, z
        if slot % 2:
            other_y = swapped(other_y, 4)
        if slot // 2:
            other_z = swapped(z, 16)
        other_y, other_z = (other_y + shift) % 4, (other_z + shift) % 16
        target = place_of(other_z % 4, x, core, other_z // 4, other_y)
        pairs.append((place_of(z_lo, x, core, z_hi, y), target))
    return lax.ppermute(value, GRID, pairs)


def dot_over(left_side, right_side, left_dim, right_dim):
    return lax.dot_general(
        left_side,
        right_side,
        (((left_dim,), (right_dim,)), ((), ())),
        preferred_element_type=jnp.float32,
    )


def copies_of(block, count):
    return jnp.broadcast_to(block[None], (count,) + block.shape)


def common_block(core, own, slot, part):
    pair = lax.bitwise_xor(own, jnp.int32(slot))
    shift = 1 - core
    y = lax.rem(lax.rem(pair, 2) * 2 + part % 2 + shift, 4)
    z = lax.rem(pair // 2 * 2 + part // 2 + shift, 4)
    return y * 4 + z


def first_kernel(p0, first, second, sums):
    width = first.shape[0]
    units = first.shape[1]
    sums[:, :units] = dot_over(p0[:, :width], first[...], 1, 0)
    sums[:, units:] = dot_over(p0[:, width:], second[...], 1, 1)


def last_kernel(place, sums, sums3, p1, p2, first, second, both, kept, given, rest):
    core, own = place[0], place[1]
    width = first.shape[0]
    units = first.shape[1]
    both[0:128, :] = p1[...]
    both[128:256, :] = p2[...]
    rest[:, :units] = dot_over(both[:, :width], first[...], 1, 0)
    rest[:, units:] = dot_over(both[:, width:], second[...], 1, 1)
    for slot in range(4):
        source, base = ((sums, 0), (rest, 1), (rest, 1), (sums3, 3))[slot]
        for part in range(4):
            block = common_block(core, own, slot, part)
            start = pl.multiple_of(lax.rem(block, 8) * BLOCK, BLOCK)
            at = ((slot - base) * 4 + part) * BLOCK
            mine = block // 8 == core

            @pl.when(mine)
            def _():
                kept[pl.ds(start, BLOCK), :] = source[at : at + BLOCK, :]

            @pl.when(jnp.logical_not(mine))
            def _():
                given[pl.ds(start, BLOCK), :] = source[at : at + BLOCK, :]


def add_kernel(kept, more, total, sent):
    values = kept[...] + more[...]
    total[...] = values
    sent[...] = values.astype(jnp.bfloat16)


def lost(values):
    return values - values.astype(jnp.bfloat16).astype(jnp.float32)


def total_of(parts, own_lost):
    wide = [parts[i].astype(jnp.float32) for i in range(4)]
    return ((wide[0] + wide[1]) + (wide[2] + wide[3])) + own_lost


def gelu_kernel(place, parts, kept, shares):
    units = shares.shape[2] // 2
    total = total_of(parts, lost(kept[place[2]]))
    values, slopes = total[:, :units], total[:, units:]
    square = values * values
    tangent = jnp.tanh(root_scale * (values + cubic_coef * values * square))
    hidden = 0.5 * values * (1.0 + tangent)
    slope = 0.5 * (1.0 + tangent) + 0.5 * values * (1.0 - tangent * tangent) * root_scale * (
        1.0 + 3.0 * cubic_coef * square
    )
    pre = slopes * slope
    for copy in range(4):
        shares[copy, :, :units] = hidden.astype(jnp.bfloat16)
        shares[copy, :, units:] = pre.astype(jnp.bfloat16)


def out_rows(rows, first, second):
    units = first.shape[1]
    return (
        dot_over(rows[:, :units], second[...], 1, 0),
        dot_over(rows[:, units:], first[...], 1, 1),
    )


def second_kernel(place, shares, first, second, o1, o2, o3, local):
    core, own = place[0], place[1]
    width = first.shape[0]
    for slot in range(4):
        for part in range(4):
            block = common_block(core, own, slot, part)
            start = pl.multiple_of(block * BLOCK, BLOCK)
            at = (slot * 4 + part) * BLOCK
            local[at : at + BLOCK, :] = shares[pl.ds(start, BLOCK), :]
    sides = out_rows(local[128:512, :], first, second)
    for side in range(2):
        outs = sides[side].astype(jnp.bfloat16)
        columns = slice(side * width, (side + 1) * width)
        o1[:, columns] = outs[0:128]
        o2[:, columns] = outs[128:256]
        o3[:, columns] = outs[256:384]


def own_kernel(local, first, second, o0):
    width = first.shape[0]
    sides = out_rows(local[0:128, :], first, second)
    o0[:, :width] = sides[0]
    o0[:, width:] = sides[1]


def far_kernel(place, r3, r1, r2, o0, outs, own_lost):
    for part in range(4):
        rows = slice(part * BLOCK, (part + 1) * BLOCK)
        total = o0[rows, :] + r1[rows, :].astype(jnp.float32)
        total = total + r2[rows, :].astype(jnp.float32) + r3[rows, :].astype(jnp.float32)
        outs[part] = total.astype(jnp.bfloat16)

        @pl.when(place[3] == part)
        def _():
            own_lost[...] = lost(total)


def near_kernel(place, parts, own_lost, outs, next_lost):
    total = total_of(parts, own_lost[...])
    outs[...] = total.astype(jnp.bfloat16)
    for part in range(4):

        @pl.when(place[4] == part)
        def _():
            next_lost[...] = lost(total[part * 8 : part * 8 + 8, :])


def end_kernel(parts, own_lost, block_out, input_grad):
    width = block_out.shape[1]
    outs = total_of(parts, own_lost[...]).astype(jnp.bfloat16)
    block_out[...] = outs[:, :width]
    input_grad[...] = outs[:, width:]


def shape_of(rows, columns, dtype):
    return jax.ShapeDtypeStruct((rows, columns), dtype)


def cost_of(rows):
    return pl.CostEstimate(
        flops=4 * rows * 1536 * 384, bytes_accessed=rows * 12288 + 2400000, transcendentals=0
    )


def on_device(tokens, first_weight, second_weight, grad_out):
    width = tokens.shape[1]
    units = first_weight.shape[1]
    core, x = lax.axis_index("core"), lax.axis_index("x")
    y, z_lo, z_hi = lax.axis_index("y"), lax.axis_index("z_lo"), lax.axis_index("z_hi")
    y, z_lo = (y + 3 + core) % 4, (z_lo + 3 + core) % 4
    own, part = z_lo // 2 * 2 + y // 2, z_lo % 2 * 2 + y % 2
    place = jnp.stack([core, own, x, part, z_hi]).astype(jnp.int32)
    scalars = pl.BlockSpec(memory_space=pltpu.SMEM)
    whole = pl.BlockSpec(memory_space=pltpu.VMEM)
    near = pair_groups()

    both = jnp.concatenate([tokens, grad_out], axis=1)
    both = lax.all_to_all(copies_of(both, 4), "z_hi", 0, 0).reshape(BLOCK, 2 * width)
    both = lax.all_to_all(copies_of(both, 4), GRID, 0, 0, axis_index_groups=near)
    both = both.reshape(PIECE, 2 * width)
    p3, p1, p2 = moved(both, 3), moved(both, 1), moved(both, 2)

    def early(rows):
        return pl.pallas_call(
            first_kernel,
            out_shape=shape_of(PIECE, 2 * units, jnp.float32),
            in_specs=[whole] * 3,
            out_specs=whole,
            compiler_params=params,
            cost_estimate=cost_of(128),
        )(rows, first_weight, second_weight)

    sums, sums3 = early(both), early(p3)
    every, kept, given = pl.pallas_call(
        last_kernel,
        out_shape=(
            shape_of(256, 2 * width, jnp.bfloat16),
            shape_of(256, 2 * units, jnp.float32),
            shape_of(256, 2 * units, jnp.float32),
        ),
        in_specs=[scalars] + [whole] * 6,
        out_specs=(whole, whole, whole),
        scratch_shapes=[pltpu.VMEM((256, 2 * units), jnp.float32)],
        compiler_params=params,
        cost_estimate=cost_of(256),
    )(place, sums, sums3, p1, p2, first_weight, second_weight)
    kept, sent = pl.pallas_call(
        add_kernel,
        out_shape=(
            shape_of(256, 2 * units, jnp.float32),
            shape_of(256, 2 * units, jnp.bfloat16),
        ),
        in_specs=[whole] * 2,
        out_specs=(whole, whole),
        compiler_params=params,
    )(kept, lax.ppermute(given, "core", SWAP))
    parts = lax.all_to_all(sent.reshape(4, SHARE, 2 * units), "x", 0, 0)
    shares = pl.pallas_call(
        gelu_kernel,
        out_shape=jax.ShapeDtypeStruct((4, SHARE, 2 * units), jnp.bfloat16),
        in_specs=[scalars, whole, whole],
        out_specs=whole,
        compiler_params=params,
    )(place, parts, kept.reshape(4, SHARE, 2 * units))
    shares = lax.all_to_all(shares, "x", 0, 0).reshape(256, 2 * units)
    shares = lax.all_gather(shares, "core", axis=0, tiled=True)
    o1, o2, o3, local = pl.pallas_call(
        second_kernel,
        out_shape=(
            shape_of(PIECE, 2 * width, jnp.bfloat16),
            shape_of(PIECE, 2 * width, jnp.bfloat16),
            shape_of(PIECE, 2 * width, jnp.bfloat16),
            shape_of(512, 2 * units, jnp.bfloat16),
        ),
        in_specs=[scalars] + [whole] * 3,
        out_specs=(whole,) * 4,
        compiler_params=params,
        cost_estimate=cost_of(384),
    )(place, shares, first_weight, second_weight)
    r3, r1, r2 = moved(o3, 3), moved(o1, 1), moved(o2, 2)
    late, r3 = lax.optimization_barrier((local, r3))
    o0 = pl.pallas_call(
        own_kernel,
        out_shape=shape_of(PIECE, 2 * width, jnp.float32),
        in_specs=[whole] * 3,
        out_specs=whole,
        compiler_params=params,
        cost_estimate=cost_of(128),
    )(late, first_weight, second_weight)
    hidden, grad_pre = local[128:384, :units], local[128:384, units:]
    late_hidden, late_pre = late[:, :units], late[:, units:]
    first_grad = dot_over(every[:, :width], grad_pre, 0, 0)
    first_grad = first_grad + dot_over(both[:, :width], late_pre[:128], 0, 0)
    first_grad = first_grad + dot_over(p3[:, :width], late_pre[384:], 0, 0)
    second_grad = dot_over(hidden, every[:, width:], 0, 0)
    second_grad = second_grad + dot_over(late_hidden[:128], both[:, width:], 0, 0)
    second_grad = second_grad + dot_over(late_hidden[384:], p3[:, width:], 0, 0)
    first_grad = first_grad.astype(jnp.bfloat16)
    second_grad = second_grad.astype(jnp.bfloat16)
    o0, first_grad, second_grad = lax.optimization_barrier((o0, first_grad, second_grad))
    outs, own_lost = pl.pallas_call(
        far_kernel,
        out_shape=(
            jax.ShapeDtypeStruct((4, BLOCK, 2 * width), jnp.bfloat16),
            shape_of(BLOCK, 2 * width, jnp.float32),
        ),
        in_specs=[scalars] + [whole] * 4,
        out_specs=(whole, whole),
        compiler_params=params,
    )(place, r3, r1, r2, o0)
    outs = lax.all_to_all(outs, GRID, 0, 0, axis_index_groups=near)
    outs, own_lost = pl.pallas_call(
        near_kernel,
        out_shape=(
            shape_of(BLOCK, 2 * width, jnp.bfloat16),
            shape_of(8, 2 * width, jnp.float32),
        ),
        in_specs=[scalars, whole, whole],
        out_specs=(whole, whole),
        compiler_params=params,
    )(place, outs, own_lost)
    outs = lax.all_to_all(outs.reshape(4, 8, 2 * width), "z_hi", 0, 0)
    block_out, input_grad = pl.pallas_call(
        end_kernel,
        out_shape=(shape_of(8, width, jnp.bfloat16), shape_of(8, width, jnp.bfloat16)),
        in_specs=[whole, whole],
        out_specs=(whole, whole),
        compiler_params=params,
    )(outs, own_lost)
    return (block_out, input_grad, first_grad, second_grad)


def solution(mesh):
    grid = Mesh(mesh.devices.reshape(SIZES), GRID)
    rows = P(("z_lo", "z_hi", "y"), ROW)
    columns = P(ROW, ("z_lo", "z_hi", "y"))
    return jax.shard_map(
        on_device,
        mesh=grid,
        in_specs=(rows, columns, rows, rows),
        out_specs=(rows, rows, columns, rows),
        check_vma=False,
    )
```

```python
import math

import jax
import jax.numpy as jnp
from jax import lax
from jax.experimental import pallas as pl
from jax.experimental.pallas import tpu as pltpu
from jax.sharding import Mesh, PartitionSpec as P

root_scale = math.sqrt(2.0 / math.pi)
cubic_coef = 0.044715

GRID = ("z_lo", "x", "core", "z_hi", "y")
SIZES = (4, 4, 2, 4, 4)
ROW = ("x", "core")
SWAP = ((0, 1), (1, 0))
BLOCK = 32
PIECE = 128
SHARE = 64
params = pltpu.CompilerParams(vmem_limit_bytes=20 << 20)


def place_of(z_lo, x, core, z_hi, y):
    return (((z_lo * 4 + x) * 2 + core) * 4 + z_hi) * 4 + y


def every_place():
    for z_lo in range(4):
        for x in range(4):
            for core in range(2):
                for z_hi in range(4):
                    for y in range(4):
                        yield z_lo, x, core, z_hi, y


def pair_groups():
    groups = []
    for x in range(4):
        for core in range(2):
            for z in range(0, 16, 2):
                for y in range(0, 4, 2):
                    group = []
                    for part in range(4):
                        real_z = (z + part // 2 + 1 - core) % 16
                        real_y = (y + part % 2 + 1 - core) % 4
                        group.append(place_of(real_z % 4, x, core, real_z // 4, real_y))
                    groups.append(group)
    return groups


def swapped(place, size):
    return (place + 1 if place % 2 else place - 1) % size


def moved(value, slot):
    pairs = []
    for z_lo, x, core, z_hi, y in every_place():
        shift = 1 - core
        z = (z_hi * 4 + z_lo - shift) % 16
        other_y, other_z = (y - shift) % 4, z
        if slot % 2:
            other_y = swapped(other_y, 4)
        if slot // 2:
            other_z = swapped(z, 16)
        other_y, other_z = (other_y + shift) % 4, (other_z + shift) % 16
        target = place_of(other_z % 4, x, core, other_z // 4, other_y)
        pairs.append((place_of(z_lo, x, core, z_hi, y), target))
    return lax.ppermute(value, GRID, pairs)


def dot_over(left_side, right_side, left_dim, right_dim):
    return lax.dot_general(
        left_side,
        right_side,
        (((left_dim,), (right_dim,)), ((), ())),
        preferred_element_type=jnp.float32,
    )


def copies_of(block, count):
    return jnp.broadcast_to(block[None], (count,) + block.shape)


def common_block(core, own, slot, part):
    pair = lax.bitwise_xor(own, jnp.int32(slot))
    odd = lax.rem(part % 2 + part // 2, 2)
    shift = 1 - core
    y = lax.rem(lax.rem(pair, 2) * 2 + part % 2 + shift, 4)
    z = lax.rem(pair // 2 * 2 + part // 2 + shift, 4)
    return odd * 8 + y * 2 + z // 2


def first_kernel(p0, first, second, sums):
    width = first.shape[0]
    units = first.shape[1]
    sums[:, :units] = dot_over(p0[:, :width], first[...], 1, 0)
    sums[:, units:] = dot_over(p0[:, width:], second[...], 1, 1)


def half_rows(place, half, sums, sums3, p1, p2, first, second, out, rows, rest):
    core, own = place[0], place[1]
    width = first.shape[0]
    units = first.shape[1]
    parts = (half, 3 - half)
    starts = [pl.multiple_of(part * BLOCK, BLOCK) for part in parts]
    for index in range(2):
        at = index * BLOCK
        rows[at : at + BLOCK, :] = p1[pl.ds(starts[index], BLOCK), :]
        rows[64 + at : 64 + at + BLOCK, :] = p2[pl.ds(starts[index], BLOCK), :]
    rest[:, :units] = dot_over(rows[:, :width], first[...], 1, 0)
    rest[:, units:] = dot_over(rows[:, width:], second[...], 1, 1)
    for index in range(2):
        for slot in range(4):
            block = common_block(core, own, slot, parts[index])
            start = pl.multiple_of(lax.rem(block, 8) * BLOCK, BLOCK)
            if slot == 0:
                values = sums[pl.ds(starts[index], BLOCK), :]
            elif slot == 3:
                values = sums3[pl.ds(starts[index], BLOCK), :]
            else:
                at = (slot - 1) * 64 + index * BLOCK
                values = rest[at : at + BLOCK, :]
            out[pl.ds(start, BLOCK), :] = values


def given_kernel(place, sums, sums3, p1, p2, first, second, given, rows, rest):
    half_rows(place, 1 - place[0], sums, sums3, p1, p2, first, second, given, rows, rest)


def kept_kernel(place, sums, sums3, p1, p2, first, second, kept, both, rows, rest):
    half_rows(place, place[0], sums, sums3, p1, p2, first, second, kept, rows, rest)
    both[0:128, :] = p1[...]
    both[128:256, :] = p2[...]


def add_kernel(kept, more, total, sent):
    values = kept[...] + more[...]
    total[...] = values
    sent[...] = values.astype(jnp.bfloat16)


def lost(values):
    return values - values.astype(jnp.bfloat16).astype(jnp.float32)


def total_of(parts, own_lost):
    wide = [parts[i].astype(jnp.float32) for i in range(4)]
    return ((wide[0] + wide[1]) + (wide[2] + wide[3])) + own_lost


def gelu_kernel(place, parts, kept, shares):
    units = shares.shape[2] // 2
    total = total_of(parts, lost(kept[place[2]]))
    values, slopes = total[:, :units], total[:, units:]
    square = values * values
    tangent = jnp.tanh(root_scale * (values + cubic_coef * values * square))
    hidden = 0.5 * values * (1.0 + tangent)
    slope = 0.5 * (1.0 + tangent) + 0.5 * values * (1.0 - tangent * tangent) * root_scale * (
        1.0 + 3.0 * cubic_coef * square
    )
    pre = slopes * slope
    for copy in range(4):
        shares[copy, :, :units] = hidden.astype(jnp.bfloat16)
        shares[copy, :, units:] = pre.astype(jnp.bfloat16)


def out_rows(rows, first, second):
    units = first.shape[1]
    return (
        dot_over(rows[:, :units], second[...], 1, 0),
        dot_over(rows[:, units:], first[...], 1, 1),
    )


def second_kernel(place, shares, first, second, o1, o2, o3, local):
    core, own = place[0], place[1]
    width = first.shape[0]
    for slot in range(4):
        for part in range(4):
            block = common_block(core, own, slot, part)
            start = pl.multiple_of(block * BLOCK, BLOCK)
            at = (slot * 4 + part) * BLOCK
            local[at : at + BLOCK, :] = shares[pl.ds(start, BLOCK), :]
    sides = out_rows(local[128:512, :], first, second)
    for side in range(2):
        outs = sides[side].astype(jnp.bfloat16)
        columns = slice(side * width, (side + 1) * width)
        o1[:, columns] = outs[0:128]
        o2[:, columns] = outs[128:256]
        o3[:, columns] = outs[256:384]


def own_kernel(local, first, second, o0):
    width = first.shape[0]
    sides = out_rows(local[0:128, :], first, second)
    o0[:, :width] = sides[0]
    o0[:, width:] = sides[1]


def far_kernel(place, r3, r1, r2, o0, outs, own_lost):
    for part in range(4):
        rows = slice(part * BLOCK, (part + 1) * BLOCK)
        total = o0[rows, :] + r1[rows, :].astype(jnp.float32)
        total = total + r2[rows, :].astype(jnp.float32) + r3[rows, :].astype(jnp.float32)
        outs[part] = total.astype(jnp.bfloat16)

        @pl.when(place[3] == part)
        def _():
            own_lost[...] = lost(total)


def near_kernel(place, parts, own_lost, outs, next_lost):
    total = total_of(parts, own_lost[...])
    outs[...] = total.astype(jnp.bfloat16)
    for part in range(4):

        @pl.when(place[4] == part)
        def _():
            next_lost[...] = lost(total[part * 8 : part * 8 + 8, :])


def end_kernel(parts, own_lost, block_out, input_grad):
    width = block_out.shape[1]
    outs = total_of(parts, own_lost[...]).astype(jnp.bfloat16)
    block_out[...] = outs[:, :width]
    input_grad[...] = outs[:, width:]


def shape_of(rows, columns, dtype):
    return jax.ShapeDtypeStruct((rows, columns), dtype)


def cost_of(rows):
    return pl.CostEstimate(
        flops=4 * rows * 1536 * 384, bytes_accessed=rows * 12288 + 2400000, transcendentals=0
    )


def on_device(tokens, first_weight, second_weight, grad_out):
    width = tokens.shape[1]
    units = first_weight.shape[1]
    core, x = lax.axis_index("core"), lax.axis_index("x")
    y, z_lo, z_hi = lax.axis_index("y"), lax.axis_index("z_lo"), lax.axis_index("z_hi")
    y, z_lo = (y + 3 + core) % 4, (z_lo + 3 + core) % 4
    own, part = z_lo // 2 * 2 + y // 2, z_lo % 2 * 2 + y % 2
    place = jnp.stack([core, own, x, part, z_hi]).astype(jnp.int32)
    scalars = pl.BlockSpec(memory_space=pltpu.SMEM)
    whole = pl.BlockSpec(memory_space=pltpu.VMEM)
    near = pair_groups()

    both = jnp.concatenate([tokens, grad_out], axis=1)
    both = lax.all_to_all(copies_of(both, 4), "z_hi", 0, 0).reshape(BLOCK, 2 * width)
    both = lax.all_to_all(copies_of(both, 4), GRID, 0, 0, axis_index_groups=near)
    both = both.reshape(PIECE, 2 * width)
    p3, p1, p2 = moved(both, 3), moved(both, 1), moved(both, 2)

    def early(rows):
        return pl.pallas_call(
            first_kernel,
            out_shape=shape_of(PIECE, 2 * units, jnp.float32),
            in_specs=[whole] * 3,
            out_specs=whole,
            compiler_params=params,
            cost_estimate=cost_of(128),
        )(rows, first_weight, second_weight)

    sums, sums3 = early(both), early(p3)
    scratch = [
        pltpu.VMEM((PIECE, 2 * width), jnp.bfloat16),
        pltpu.VMEM((PIECE, 2 * units), jnp.float32),
    ]
    inputs = (place, sums, sums3, p1, p2, first_weight, second_weight)
    given = pl.pallas_call(
        given_kernel,
        out_shape=shape_of(256, 2 * units, jnp.float32),
        in_specs=[scalars] + [whole] * 6,
        out_specs=whole,
        scratch_shapes=scratch,
        compiler_params=params,
        cost_estimate=cost_of(128),
    )(*inputs)
    more = lax.ppermute(given, "core", SWAP)
    kept, every = pl.pallas_call(
        kept_kernel,
        out_shape=(
            shape_of(256, 2 * units, jnp.float32),
            shape_of(256, 2 * width, jnp.bfloat16),
        ),
        in_specs=[scalars] + [whole] * 6,
        out_specs=(whole, whole),
        scratch_shapes=scratch,
        compiler_params=params,
        cost_estimate=cost_of(128),
    )(*inputs)
    kept, sent = pl.pallas_call(
        add_kernel,
        out_shape=(
            shape_of(256, 2 * units, jnp.float32),
            shape_of(256, 2 * units, jnp.bfloat16),
        ),
        in_specs=[whole] * 2,
        out_specs=(whole, whole),
        compiler_params=params,
    )(kept, more)
    parts = lax.all_to_all(sent.reshape(4, SHARE, 2 * units), "x", 0, 0)
    shares = pl.pallas_call(
        gelu_kernel,
        out_shape=jax.ShapeDtypeStruct((4, SHARE, 2 * units), jnp.bfloat16),
        in_specs=[scalars, whole, whole],
        out_specs=whole,
        compiler_params=params,
    )(place, parts, kept.reshape(4, SHARE, 2 * units))
    shares = lax.all_to_all(shares, "x", 0, 0).reshape(256, 2 * units)
    shares = lax.all_gather(shares, "core", axis=0, tiled=True)
    o1, o2, o3, local = pl.pallas_call(
        second_kernel,
        out_shape=(
            shape_of(PIECE, 2 * width, jnp.bfloat16),
            shape_of(PIECE, 2 * width, jnp.bfloat16),
            shape_of(PIECE, 2 * width, jnp.bfloat16),
            shape_of(512, 2 * units, jnp.bfloat16),
        ),
        in_specs=[scalars] + [whole] * 3,
        out_specs=(whole,) * 4,
        compiler_params=params,
        cost_estimate=cost_of(384),
    )(place, shares, first_weight, second_weight)
    r3, r1, r2 = moved(o3, 3), moved(o1, 1), moved(o2, 2)
    late, r3 = lax.optimization_barrier((local, r3))
    o0 = pl.pallas_call(
        own_kernel,
        out_shape=shape_of(PIECE, 2 * width, jnp.float32),
        in_specs=[whole] * 3,
        out_specs=whole,
        compiler_params=params,
        cost_estimate=cost_of(128),
    )(late, first_weight, second_weight)
    hidden, grad_pre = local[128:384, :units], local[128:384, units:]
    late_hidden, late_pre = late[:, :units], late[:, units:]
    first_grad = dot_over(every[:, :width], grad_pre, 0, 0)
    first_grad = first_grad + dot_over(both[:, :width], late_pre[:128], 0, 0)
    first_grad = first_grad + dot_over(p3[:, :width], late_pre[384:], 0, 0)
    second_grad = dot_over(hidden, every[:, width:], 0, 0)
    second_grad = second_grad + dot_over(late_hidden[:128], both[:, width:], 0, 0)
    second_grad = second_grad + dot_over(late_hidden[384:], p3[:, width:], 0, 0)
    first_grad = first_grad.astype(jnp.bfloat16)
    second_grad = second_grad.astype(jnp.bfloat16)
    o0, first_grad, second_grad = lax.optimization_barrier((o0, first_grad, second_grad))
    outs, own_lost = pl.pallas_call(
        far_kernel,
        out_shape=(
            jax.ShapeDtypeStruct((4, BLOCK, 2 * width), jnp.bfloat16),
            shape_of(BLOCK, 2 * width, jnp.float32),
        ),
        in_specs=[scalars] + [whole] * 4,
        out_specs=(whole, whole),
        compiler_params=params,
    )(place, r3, r1, r2, o0)
    outs = lax.all_to_all(outs, GRID, 0, 0, axis_index_groups=near)
    outs, own_lost = pl.pallas_call(
        near_kernel,
        out_shape=(
            shape_of(BLOCK, 2 * width, jnp.bfloat16),
            shape_of(8, 2 * width, jnp.float32),
        ),
        in_specs=[scalars, whole, whole],
        out_specs=(whole, whole),
        compiler_params=params,
    )(place, outs, own_lost)
    outs = lax.all_to_all(outs.reshape(4, 8, 2 * width), "z_hi", 0, 0)
    block_out, input_grad = pl.pallas_call(
        end_kernel,
        out_shape=(shape_of(8, width, jnp.bfloat16), shape_of(8, width, jnp.bfloat16)),
        in_specs=[whole, whole],
        out_specs=(whole, whole),
        compiler_params=params,
    )(outs, own_lost)
    return (block_out, input_grad, first_grad, second_grad)


def solution(mesh):
    grid = Mesh(mesh.devices.reshape(SIZES), GRID)
    rows = P(("z_lo", "z_hi", "y"), ROW)
    columns = P(ROW, ("z_lo", "z_hi", "y"))
    return jax.shard_map(
        on_device,
        mesh=grid,
        in_specs=(rows, columns, rows, rows),
        out_specs=(rows, rows, columns, rows),
        check_vma=False,
    )
```

```python
import math

import jax
import jax.numpy as jnp
from jax import lax
from jax.experimental import pallas as pl
from jax.experimental.pallas import tpu as pltpu
from jax.sharding import Mesh, PartitionSpec as P

root_scale = math.sqrt(2.0 / math.pi)
cubic_coef = 0.044715

GRID = ("z_lo", "x", "core", "z_hi", "y")
SIZES = (4, 4, 2, 4, 4)
ROW = ("x", "core")
SWAP = ((0, 1), (1, 0))
BLOCK = 32
PIECE = 128
SHARE = 64
params = pltpu.CompilerParams(vmem_limit_bytes=20 << 20)


def place_of(z_lo, x, core, z_hi, y):
    return (((z_lo * 4 + x) * 2 + core) * 4 + z_hi) * 4 + y


def every_place():
    for z_lo in range(4):
        for x in range(4):
            for core in range(2):
                for z_hi in range(4):
                    for y in range(4):
                        yield z_lo, x, core, z_hi, y


def pair_groups():
    groups = []
    for x in range(4):
        for core in range(2):
            for z in range(0, 16, 2):
                for y in range(0, 4, 2):
                    group = []
                    for part in range(4):
                        real_z = (z + part // 2 + 1 - core) % 16
                        real_y = (y + part % 2 + 1 - core) % 4
                        group.append(place_of(real_z % 4, x, core, real_z // 4, real_y))
                    groups.append(group)
    return groups


def swapped(place, size):
    return (place + 1 if place % 2 else place - 1) % size


def moved(value, slot):
    pairs = []
    for z_lo, x, core, z_hi, y in every_place():
        shift = 1 - core
        z = (z_hi * 4 + z_lo - shift) % 16
        other_y, other_z = (y - shift) % 4, z
        if slot % 2:
            other_y = swapped(other_y, 4)
        if slot // 2:
            other_z = swapped(z, 16)
        other_y, other_z = (other_y + shift) % 4, (other_z + shift) % 16
        target = place_of(other_z % 4, x, core, other_z // 4, other_y)
        pairs.append((place_of(z_lo, x, core, z_hi, y), target))
    return lax.ppermute(value, GRID, pairs)


def dot_over(left_side, right_side, left_dim, right_dim):
    return lax.dot_general(
        left_side,
        right_side,
        (((left_dim,), (right_dim,)), ((), ())),
        preferred_element_type=jnp.float32,
    )


def copies_of(block, count):
    return jnp.broadcast_to(block[None], (count,) + block.shape)


def common_block(core, own, slot, part):
    pair = lax.bitwise_xor(own, jnp.int32(slot))
    shift = 1 - core
    y = lax.rem(lax.rem(pair, 2) * 2 + part % 2 + shift, 4)
    z = lax.rem(pair // 2 * 2 + part // 2 + shift, 4)
    return y * 4 + z


def first_kernel(p0, first, second, sums):
    width = first.shape[0]
    units = first.shape[1]
    sums[:, :units] = dot_over(p0[:, :width], first[...], 1, 0)
    sums[:, units:] = dot_over(p0[:, width:], second[...], 1, 1)


def last_kernel(place, sums, sums3, p1, p2, first, second, both, kept, given, rest):
    core, own = place[0], place[1]
    width = first.shape[0]
    units = first.shape[1]
    both[0:128, :] = p1[...]
    both[128:256, :] = p2[...]
    rest[:, :units] = dot_over(both[:, :width], first[...], 1, 0)
    rest[:, units:] = dot_over(both[:, width:], second[...], 1, 1)
    for slot in range(4):
        source, base = ((sums, 0), (rest, 1), (rest, 1), (sums3, 3))[slot]
        for part in range(4):
            block = common_block(core, own, slot, part)
            start = pl.multiple_of(lax.rem(block, 8) * BLOCK, BLOCK)
            at = ((slot - base) * 4 + part) * BLOCK
            mine = block // 8 == core

            @pl.when(mine)
            def _():
                kept[pl.ds(start, BLOCK), :] = source[at : at + BLOCK, :]

            @pl.when(jnp.logical_not(mine))
            def _():
                given[pl.ds(start, BLOCK), :] = source[at : at + BLOCK, :]


def add_kernel(kept, more, total, sent):
    values = kept[...] + more[...]
    total[...] = values
    sent[...] = values.astype(jnp.bfloat16)


def lost(values):
    return values - values.astype(jnp.bfloat16).astype(jnp.float32)


def total_of(parts, own_lost):
    wide = [parts[i].astype(jnp.float32) for i in range(4)]
    return ((wide[0] + wide[1]) + (wide[2] + wide[3])) + own_lost


def gelu_kernel(place, parts, kept, shares):
    units = shares.shape[2] // 2
    total = total_of(parts, lost(kept[place[2]]))
    values, slopes = total[:, :units], total[:, units:]
    square = values * values
    tangent = jnp.tanh(root_scale * (values + cubic_coef * values * square))
    hidden = 0.5 * values * (1.0 + tangent)
    slope = 0.5 * (1.0 + tangent) + 0.5 * values * (1.0 - tangent * tangent) * root_scale * (
        1.0 + 3.0 * cubic_coef * square
    )
    pre = slopes * slope
    for copy in range(4):
        shares[copy, :, :units] = hidden.astype(jnp.bfloat16)
        shares[copy, :, units:] = pre.astype(jnp.bfloat16)


def out_rows(rows, first, second):
    units = first.shape[1]
    return (
        dot_over(rows[:, :units], second[...], 1, 0),
        dot_over(rows[:, units:], first[...], 1, 1),
    )


def second_kernel(place, shares, first, second, o1, o2, o3, local):
    core, own = place[0], place[1]
    width = first.shape[0]
    for slot in range(4):
        for part in range(4):
            block = common_block(core, own, slot, part)
            start = pl.multiple_of(block * BLOCK, BLOCK)
            at = (slot * 4 + part) * BLOCK
            local[at : at + BLOCK, :] = shares[pl.ds(start, BLOCK), :]
    sides = out_rows(local[128:512, :], first, second)
    for side in range(2):
        outs = sides[side].astype(jnp.bfloat16)
        columns = slice(side * width, (side + 1) * width)
        o1[:, columns] = outs[0:128]
        o2[:, columns] = outs[128:256]
        o3[:, columns] = outs[256:384]


def own_kernel(local, first, second, r3, o0):
    width = first.shape[0]
    sides = out_rows(local[0:128, :], first, second)
    o0[:, :width] = sides[0] + r3[:, :width].astype(jnp.float32)
    o0[:, width:] = sides[1] + r3[:, width:].astype(jnp.float32)


def far_kernel(place, r1, r2, o0, outs, own_lost):
    for part in range(4):
        rows = slice(part * BLOCK, (part + 1) * BLOCK)
        total = o0[rows, :] + r1[rows, :].astype(jnp.float32)
        total = total + r2[rows, :].astype(jnp.float32)
        outs[part] = total.astype(jnp.bfloat16)

        @pl.when(place[3] == part)
        def _():
            own_lost[...] = lost(total)


def near_kernel(place, parts, own_lost, outs, next_lost):
    total = total_of(parts, own_lost[...])
    outs[...] = total.astype(jnp.bfloat16)
    for part in range(4):

        @pl.when(place[4] == part)
        def _():
            next_lost[...] = lost(total[part * 8 : part * 8 + 8, :])


def end_kernel(parts, own_lost, block_out, input_grad):
    width = block_out.shape[1]
    outs = total_of(parts, own_lost[...]).astype(jnp.bfloat16)
    block_out[...] = outs[:, :width]
    input_grad[...] = outs[:, width:]


def shape_of(rows, columns, dtype):
    return jax.ShapeDtypeStruct((rows, columns), dtype)


def cost_of(rows):
    return pl.CostEstimate(
        flops=4 * rows * 1536 * 384, bytes_accessed=rows * 12288 + 2400000, transcendentals=0
    )


def on_device(tokens, first_weight, second_weight, grad_out):
    width = tokens.shape[1]
    units = first_weight.shape[1]
    core, x = lax.axis_index("core"), lax.axis_index("x")
    y, z_lo, z_hi = lax.axis_index("y"), lax.axis_index("z_lo"), lax.axis_index("z_hi")
    y, z_lo = (y + 3 + core) % 4, (z_lo + 3 + core) % 4
    own, part = z_lo // 2 * 2 + y // 2, z_lo % 2 * 2 + y % 2
    place = jnp.stack([core, own, x, part, z_hi]).astype(jnp.int32)
    scalars = pl.BlockSpec(memory_space=pltpu.SMEM)
    whole = pl.BlockSpec(memory_space=pltpu.VMEM)
    near = pair_groups()

    both = jnp.concatenate([tokens, grad_out], axis=1)
    both = lax.all_to_all(copies_of(both, 4), "z_hi", 0, 0).reshape(BLOCK, 2 * width)
    both = lax.all_to_all(copies_of(both, 4), GRID, 0, 0, axis_index_groups=near)
    both = both.reshape(PIECE, 2 * width)
    p3, p1, p2 = moved(both, 3), moved(both, 1), moved(both, 2)

    def early(rows):
        return pl.pallas_call(
            first_kernel,
            out_shape=shape_of(PIECE, 2 * units, jnp.float32),
            in_specs=[whole] * 3,
            out_specs=whole,
            compiler_params=params,
            cost_estimate=cost_of(128),
        )(rows, first_weight, second_weight)

    sums, sums3 = early(both), early(p3)
    every, kept, given = pl.pallas_call(
        last_kernel,
        out_shape=(
            shape_of(256, 2 * width, jnp.bfloat16),
            shape_of(256, 2 * units, jnp.float32),
            shape_of(256, 2 * units, jnp.float32),
        ),
        in_specs=[scalars] + [whole] * 6,
        out_specs=(whole, whole, whole),
        scratch_shapes=[pltpu.VMEM((256, 2 * units), jnp.float32)],
        compiler_params=params,
        cost_estimate=cost_of(256),
    )(place, sums, sums3, p1, p2, first_weight, second_weight)
    kept, sent = pl.pallas_call(
        add_kernel,
        out_shape=(
            shape_of(256, 2 * units, jnp.float32),
            shape_of(256, 2 * units, jnp.bfloat16),
        ),
        in_specs=[whole] * 2,
        out_specs=(whole, whole),
        compiler_params=params,
    )(kept, lax.ppermute(given, "core", SWAP))
    parts = lax.all_to_all(sent.reshape(4, SHARE, 2 * units), "x", 0, 0)
    shares = pl.pallas_call(
        gelu_kernel,
        out_shape=jax.ShapeDtypeStruct((4, SHARE, 2 * units), jnp.bfloat16),
        in_specs=[scalars, whole, whole],
        out_specs=whole,
        compiler_params=params,
    )(place, parts, kept.reshape(4, SHARE, 2 * units))
    shares = lax.all_to_all(shares, "x", 0, 0).reshape(256, 2 * units)
    shares = lax.all_gather(shares, "core", axis=0, tiled=True)
    o1, o2, o3, local = pl.pallas_call(
        second_kernel,
        out_shape=(
            shape_of(PIECE, 2 * width, jnp.bfloat16),
            shape_of(PIECE, 2 * width, jnp.bfloat16),
            shape_of(PIECE, 2 * width, jnp.bfloat16),
            shape_of(512, 2 * units, jnp.bfloat16),
        ),
        in_specs=[scalars] + [whole] * 3,
        out_specs=(whole,) * 4,
        compiler_params=params,
        cost_estimate=cost_of(384),
    )(place, shares, first_weight, second_weight)
    r3, r1, r2 = moved(o3, 3), moved(o1, 1), moved(o2, 2)
    late, r3 = lax.optimization_barrier((local, r3))
    o0 = pl.pallas_call(
        own_kernel,
        out_shape=shape_of(PIECE, 2 * width, jnp.float32),
        in_specs=[whole] * 4,
        out_specs=whole,
        compiler_params=params,
        cost_estimate=cost_of(128),
    )(late, first_weight, second_weight, r3)
    hidden, grad_pre = local[128:384, :units], local[128:384, units:]
    late_hidden, late_pre = late[:, :units], late[:, units:]
    first_grad = dot_over(every[:, :width], grad_pre, 0, 0)
    first_grad = first_grad + dot_over(both[:, :width], late_pre[:128], 0, 0)
    first_grad = first_grad + dot_over(p3[:, :width], late_pre[384:], 0, 0)
    second_grad = dot_over(hidden, every[:, width:], 0, 0)
    second_grad = second_grad + dot_over(late_hidden[:128], both[:, width:], 0, 0)
    second_grad = second_grad + dot_over(late_hidden[384:], p3[:, width:], 0, 0)
    first_grad = first_grad.astype(jnp.bfloat16)
    second_grad = second_grad.astype(jnp.bfloat16)
    o0, first_grad, second_grad = lax.optimization_barrier((o0, first_grad, second_grad))
    outs, own_lost = pl.pallas_call(
        far_kernel,
        out_shape=(
            jax.ShapeDtypeStruct((4, BLOCK, 2 * width), jnp.bfloat16),
            shape_of(BLOCK, 2 * width, jnp.float32),
        ),
        in_specs=[scalars] + [whole] * 3,
        out_specs=(whole, whole),
        compiler_params=params,
    )(place, r1, r2, o0)
    outs = lax.all_to_all(outs, GRID, 0, 0, axis_index_groups=near)
    outs, own_lost = pl.pallas_call(
        near_kernel,
        out_shape=(
            shape_of(BLOCK, 2 * width, jnp.bfloat16),
            shape_of(8, 2 * width, jnp.float32),
        ),
        in_specs=[scalars, whole, whole],
        out_specs=(whole, whole),
        compiler_params=params,
    )(place, outs, own_lost)
    outs = lax.all_to_all(outs.reshape(4, 8, 2 * width), "z_hi", 0, 0)
    block_out, input_grad = pl.pallas_call(
        end_kernel,
        out_shape=(shape_of(8, width, jnp.bfloat16), shape_of(8, width, jnp.bfloat16)),
        in_specs=[whole, whole],
        out_specs=(whole, whole),
        compiler_params=params,
    )(outs, own_lost)
    return (block_out, input_grad, first_grad, second_grad)


def solution(mesh):
    grid = Mesh(mesh.devices.reshape(SIZES), GRID)
    rows = P(("z_lo", "z_hi", "y"), ROW)
    columns = P(ROW, ("z_lo", "z_hi", "y"))
    return jax.shard_map(
        on_device,
        mesh=grid,
        in_specs=(rows, columns, rows, rows),
        out_specs=(rows, rows, columns, rows),
        check_vma=False,
    )
```

```python
import math

import jax
import jax.numpy as jnp
from jax import lax
from jax.experimental import pallas as pl
from jax.experimental.pallas import tpu as pltpu
from jax.sharding import Mesh, PartitionSpec as P

root_scale = math.sqrt(2.0 / math.pi)
cubic_coef = 0.044715

GRID = ("z_lo", "x", "core", "z_hi", "y")
SIZES = (4, 4, 2, 4, 4)
ROW = ("x", "core")
SWAP = ((0, 1), (1, 0))
BLOCK = 32
PIECE = 128
SHARE = 64
params = pltpu.CompilerParams(vmem_limit_bytes=20 << 20)


def place_of(z_lo, x, core, z_hi, y):
    return (((z_lo * 4 + x) * 2 + core) * 4 + z_hi) * 4 + y


def every_place():
    for z_lo in range(4):
        for x in range(4):
            for core in range(2):
                for z_hi in range(4):
                    for y in range(4):
                        yield z_lo, x, core, z_hi, y


def pair_groups():
    groups = []
    for x in range(4):
        for core in range(2):
            for z in range(0, 16, 2):
                for y in range(0, 4, 2):
                    group = []
                    for part in range(4):
                        real_z = (z + part // 2 + 1 - core) % 16
                        real_y = (y + part % 2 + 1 - core) % 4
                        group.append(place_of(real_z % 4, x, core, real_z // 4, real_y))
                    groups.append(group)
    return groups


def swapped(place, size):
    return (place + 1 if place % 2 else place - 1) % size


def moved(value, slot):
    pairs = []
    for z_lo, x, core, z_hi, y in every_place():
        shift = 1 - core
        z = (z_hi * 4 + z_lo - shift) % 16
        other_y, other_z = (y - shift) % 4, z
        if slot % 2:
            other_y = swapped(other_y, 4)
        if slot // 2:
            other_z = swapped(z, 16)
        other_y, other_z = (other_y + shift) % 4, (other_z + shift) % 16
        target = place_of(other_z % 4, x, core, other_z // 4, other_y)
        pairs.append((place_of(z_lo, x, core, z_hi, y), target))
    return lax.ppermute(value, GRID, pairs)


def dot_over(left_side, right_side, left_dim, right_dim):
    return lax.dot_general(
        left_side,
        right_side,
        (((left_dim,), (right_dim,)), ((), ())),
        preferred_element_type=jnp.float32,
    )


def copies_of(block, count):
    return jnp.broadcast_to(block[None], (count,) + block.shape)


def common_block(core, own, slot, part):
    pair = lax.bitwise_xor(own, jnp.int32(slot))
    shift = 1 - core
    y = lax.rem(lax.rem(pair, 2) * 2 + part % 2 + shift, 4)
    z = lax.rem(pair // 2 * 2 + part // 2 + shift, 4)
    return y * 4 + z


def first_kernel(p0, first, second, sums):
    width = first.shape[0]
    units = first.shape[1]
    sums[:, :units] = dot_over(p0[:, :width], first[...], 1, 0)
    sums[:, units:] = dot_over(p0[:, width:], second[...], 1, 1)


def last_kernel(place, sums, sums3, p1, p2, first, second, both, kept, given, rest):
    core, own = place[0], place[1]
    width = first.shape[0]
    units = first.shape[1]
    both[0:128, :] = p1[...]
    both[128:256, :] = p2[...]
    rest[:, :units] = dot_over(both[:, :width], first[...], 1, 0)
    rest[:, units:] = dot_over(both[:, width:], second[...], 1, 1)
    for slot in range(4):
        source, base = ((sums, 0), (rest, 1), (rest, 1), (sums3, 3))[slot]
        for part in range(4):
            block = common_block(core, own, slot, part)
            start = pl.multiple_of(lax.rem(block, 8) * BLOCK, BLOCK)
            at = ((slot - base) * 4 + part) * BLOCK
            mine = block // 8 == core

            @pl.when(mine)
            def _():
                kept[pl.ds(start, BLOCK), :] = source[at : at + BLOCK, :]

            @pl.when(jnp.logical_not(mine))
            def _():
                given[pl.ds(start, BLOCK), :] = source[at : at + BLOCK, :]


def add_kernel(kept, more, total, sent):
    values = kept[...] + more[...]
    total[...] = values
    sent[...] = values.astype(jnp.bfloat16)


def lost(values):
    return values - values.astype(jnp.bfloat16).astype(jnp.float32)


def total_of(parts, own_lost):
    wide = [parts[i].astype(jnp.float32) for i in range(4)]
    return ((wide[0] + wide[1]) + (wide[2] + wide[3])) + own_lost


def gelu_kernel(place, parts, kept, shares):
    units = shares.shape[2] // 2
    total = total_of(parts, lost(kept[place[2]]))
    values, slopes = total[:, :units], total[:, units:]
    square = values * values
    tangent = jnp.tanh(root_scale * (values + cubic_coef * values * square))
    hidden = 0.5 * values * (1.0 + tangent)
    slope = 0.5 * (1.0 + tangent) + 0.5 * values * (1.0 - tangent * tangent) * root_scale * (
        1.0 + 3.0 * cubic_coef * square
    )
    pre = slopes * slope
    for copy in range(4):
        shares[copy, :, :units] = hidden.astype(jnp.bfloat16)
        shares[copy, :, units:] = pre.astype(jnp.bfloat16)


def out_rows(rows, first, second):
    units = first.shape[1]
    return (
        dot_over(rows[:, :units], second[...], 1, 0),
        dot_over(rows[:, units:], first[...], 1, 1),
    )


def second_kernel(place, shares, first, second, o1, o2, o3, local):
    core, own = place[0], place[1]
    width = first.shape[0]
    for slot in range(4):
        for part in range(4):
            block = common_block(core, own, slot, part)
            start = pl.multiple_of(block * BLOCK, BLOCK)
            at = (slot * 4 + part) * BLOCK
            local[at : at + BLOCK, :] = shares[pl.ds(start, BLOCK), :]
    sides = out_rows(local[128:512, :], first, second)
    for side in range(2):
        outs = sides[side].astype(jnp.bfloat16)
        columns = slice(side * width, (side + 1) * width)
        o1[:, columns] = outs[0:128]
        o2[:, columns] = outs[128:256]
        o3[:, columns] = outs[256:384]


def own_kernel(local, first, second, o0):
    width = first.shape[0]
    sides = out_rows(local[0:128, :], first, second)
    o0[:, :width] = sides[0]
    o0[:, width:] = sides[1]


def far_kernel(place, r3, r1, r2, o0, outs, own_lost):
    for part in range(4):
        rows = slice(part * BLOCK, (part + 1) * BLOCK)
        total = o0[rows, :] + r1[rows, :].astype(jnp.float32)
        total = total + r2[rows, :].astype(jnp.float32) + r3[rows, :].astype(jnp.float32)
        outs[part] = total.astype(jnp.bfloat16)

        @pl.when(place[3] == part)
        def _():
            own_lost[...] = lost(total)


def near_kernel(parts, own_lost, outs):
    outs[...] = total_of(parts, own_lost[...]).astype(jnp.bfloat16)


def end_kernel(parts, block_out, input_grad):
    width = block_out.shape[1]
    wide = [parts[i].astype(jnp.float32) for i in range(4)]
    outs = ((wide[0] + wide[1]) + (wide[2] + wide[3])).astype(jnp.bfloat16)
    block_out[...] = outs[:, :width]
    input_grad[...] = outs[:, width:]


def shape_of(rows, columns, dtype):
    return jax.ShapeDtypeStruct((rows, columns), dtype)


def cost_of(rows):
    return pl.CostEstimate(
        flops=4 * rows * 1536 * 384, bytes_accessed=rows * 12288 + 2400000, transcendentals=0
    )


def on_device(tokens, first_weight, second_weight, grad_out):
    width = tokens.shape[1]
    units = first_weight.shape[1]
    core, x = lax.axis_index("core"), lax.axis_index("x")
    y, z_lo, z_hi = lax.axis_index("y"), lax.axis_index("z_lo"), lax.axis_index("z_hi")
    y, z_lo = (y + 3 + core) % 4, (z_lo + 3 + core) % 4
    own, part = z_lo // 2 * 2 + y // 2, z_lo % 2 * 2 + y % 2
    place = jnp.stack([core, own, x, part, z_hi]).astype(jnp.int32)
    scalars = pl.BlockSpec(memory_space=pltpu.SMEM)
    whole = pl.BlockSpec(memory_space=pltpu.VMEM)
    near = pair_groups()

    both = jnp.concatenate([tokens, grad_out], axis=1)
    both = lax.all_to_all(copies_of(both, 4), "z_hi", 0, 0).reshape(BLOCK, 2 * width)
    both = lax.all_to_all(copies_of(both, 4), GRID, 0, 0, axis_index_groups=near)
    both = both.reshape(PIECE, 2 * width)
    p3, p1, p2 = moved(both, 3), moved(both, 1), moved(both, 2)

    def early(rows):
        return pl.pallas_call(
            first_kernel,
            out_shape=shape_of(PIECE, 2 * units, jnp.float32),
            in_specs=[whole] * 3,
            out_specs=whole,
            compiler_params=params,
            cost_estimate=cost_of(128),
        )(rows, first_weight, second_weight)

    sums, sums3 = early(both), early(p3)
    every, kept, given = pl.pallas_call(
        last_kernel,
        out_shape=(
            shape_of(256, 2 * width, jnp.bfloat16),
            shape_of(256, 2 * units, jnp.float32),
            shape_of(256, 2 * units, jnp.float32),
        ),
        in_specs=[scalars] + [whole] * 6,
        out_specs=(whole, whole, whole),
        scratch_shapes=[pltpu.VMEM((256, 2 * units), jnp.float32)],
        compiler_params=params,
        cost_estimate=cost_of(256),
    )(place, sums, sums3, p1, p2, first_weight, second_weight)
    kept, sent = pl.pallas_call(
        add_kernel,
        out_shape=(
            shape_of(256, 2 * units, jnp.float32),
            shape_of(256, 2 * units, jnp.bfloat16),
        ),
        in_specs=[whole] * 2,
        out_specs=(whole, whole),
        compiler_params=params,
    )(kept, lax.ppermute(given, "core", SWAP))
    parts = lax.all_to_all(sent.reshape(4, SHARE, 2 * units), "x", 0, 0)
    shares = pl.pallas_call(
        gelu_kernel,
        out_shape=jax.ShapeDtypeStruct((4, SHARE, 2 * units), jnp.bfloat16),
        in_specs=[scalars, whole, whole],
        out_specs=whole,
        compiler_params=params,
    )(place, parts, kept.reshape(4, SHARE, 2 * units))
    shares = lax.all_to_all(shares, "x", 0, 0).reshape(256, 2 * units)
    shares = lax.all_gather(shares, "core", axis=0, tiled=True)
    o1, o2, o3, local = pl.pallas_call(
        second_kernel,
        out_shape=(
            shape_of(PIECE, 2 * width, jnp.bfloat16),
            shape_of(PIECE, 2 * width, jnp.bfloat16),
            shape_of(PIECE, 2 * width, jnp.bfloat16),
            shape_of(512, 2 * units, jnp.bfloat16),
        ),
        in_specs=[scalars] + [whole] * 3,
        out_specs=(whole,) * 4,
        compiler_params=params,
        cost_estimate=cost_of(384),
    )(place, shares, first_weight, second_weight)
    r3, r1, r2 = moved(o3, 3), moved(o1, 1), moved(o2, 2)
    late, r3 = lax.optimization_barrier((local, r3))
    o0 = pl.pallas_call(
        own_kernel,
        out_shape=shape_of(PIECE, 2 * width, jnp.float32),
        in_specs=[whole] * 3,
        out_specs=whole,
        compiler_params=params,
        cost_estimate=cost_of(128),
    )(late, first_weight, second_weight)
    hidden, grad_pre = local[128:384, :units], local[128:384, units:]
    late_hidden, late_pre = late[:, :units], late[:, units:]
    first_grad = dot_over(every[:, :width], grad_pre, 0, 0)
    first_grad = first_grad + dot_over(both[:, :width], late_pre[:128], 0, 0)
    first_grad = first_grad + dot_over(p3[:, :width], late_pre[384:], 0, 0)
    second_grad = dot_over(hidden, every[:, width:], 0, 0)
    second_grad = second_grad + dot_over(late_hidden[:128], both[:, width:], 0, 0)
    second_grad = second_grad + dot_over(late_hidden[384:], p3[:, width:], 0, 0)
    first_grad = first_grad.astype(jnp.bfloat16)
    second_grad = second_grad.astype(jnp.bfloat16)
    o0, first_grad, second_grad = lax.optimization_barrier((o0, first_grad, second_grad))
    outs, own_lost = pl.pallas_call(
        far_kernel,
        out_shape=(
            jax.ShapeDtypeStruct((4, BLOCK, 2 * width), jnp.bfloat16),
            shape_of(BLOCK, 2 * width, jnp.float32),
        ),
        in_specs=[scalars] + [whole] * 4,
        out_specs=(whole, whole),
        compiler_params=params,
    )(place, r3, r1, r2, o0)
    outs = lax.all_to_all(outs, GRID, 0, 0, axis_index_groups=near)
    outs = pl.pallas_call(
        near_kernel,
        out_shape=shape_of(BLOCK, 2 * width, jnp.bfloat16),
        in_specs=[whole, whole],
        out_specs=whole,
        compiler_params=params,
    )(outs, own_lost)
    outs = lax.all_to_all(outs.reshape(4, 8, 2 * width), "z_hi", 0, 0)
    block_out, input_grad = pl.pallas_call(
        end_kernel,
        out_shape=(shape_of(8, width, jnp.bfloat16), shape_of(8, width, jnp.bfloat16)),
        in_specs=[whole],
        out_specs=(whole, whole),
        compiler_params=params,
    )(outs)
    return (block_out, input_grad, first_grad, second_grad)


def solution(mesh):
    grid = Mesh(mesh.devices.reshape(SIZES), GRID)
    rows = P(("z_lo", "z_hi", "y"), ROW)
    columns = P(ROW, ("z_lo", "z_hi", "y"))
    return jax.shard_map(
        on_device,
        mesh=grid,
        in_specs=(rows, columns, rows, rows),
        out_specs=(rows, rows, columns, rows),
        check_vma=False,
    )
```
